128 devices in a mesh: seq: 32 (over z, x, core), head: 4 (over y).
Axes of the slice: x: 4, y: 4, z: 4, core: 2. Of those that a mesh axis runs over, the one named last changes fastest.
Arguments:
- queries: bfloat16 [32768, 1024], P('seq', 'head'), may hold values from -0.14941406 to 0.14941406
- key_rows: bfloat16 [32768, 1024], P('seq', 'head'), may hold values from -0.14941406 to 0.14941406
- value_rows: bfloat16 [32768, 1024], P('seq', 'head'), may hold values from -0.14941406 to 0.14941406
- grad_out: bfloat16 [32768, 1024], P('seq', 'head'), may hold values from -6 to 6
- accepted: int32 [32768], P('seq'), may hold values 0 or 1
- decay_code: int32 [8], P('head'), may hold values from 14 to 40
- w_query: bfloat16 [6144, 1024], P(None, 'head'), may hold values from -0.078125 to 0.078125
- w_key: bfloat16 [6144, 1024], P(None, 'head'), may hold values from -0.078125 to 0.078125
- w_value: bfloat16 [6144, 1024], P(None, 'head'), may hold values from -0.078125 to 0.078125
Outputs:
- input_grad: bfloat16 [32768, 6144], P('seq', 'head')
The draws below stay inside these ranges and needn't reach their ends.
All inputs are finite; a program needn't handle non-finite values. No bound on the sum of `accepted` on one device may be relied on, other than what follows from the above.
Results may differ from the reference program's by a relative error of at most 0.015.
Values may be sent and summed in bfloat16 or wider, within the bound.
No kernel may reach another device: no remote copies, remote signals or barrier semaphores. Data moves between devices by JAX's collectives and lax.ppermute only.
A program may use at most 192 MiB of HBM per device.

```python
import jax
import jax.numpy as jnp
from jax import lax

D = 6144
HDIM = 128
GROUP = 256
HEADS = 8
TOKENS = 32768


def plant(drawn, key, low, largest):
    longest = drawn.shape.index(max(drawn.shape))
    spots = []
    for shift in (0, 1):
        where = [jax.random.randint(jax.random.fold_in(key, axis), (), 0, length) for axis, length in enumerate(drawn.shape)]
        where[longest] = (where[longest] + shift) % drawn.shape[longest]
        spots.append(tuple(where))
    return drawn.at[spots[0]].set(low).at[spots[1]].set(largest)


def shard_levels(stream_key, shape, shards, smallest, largest):
    level, own = 1.0, jax.random.fold_in(stream_key, 6)
    for position, blocks in shards:
        heights = jnp.exp(jax.random.uniform(jax.random.fold_in(own, position), (blocks,), jnp.float32, smallest / len(shards), largest / len(shards)))
        level = level * jnp.repeat(heights, shape[position] // blocks).reshape([-1 if axis == position else 1 for axis in range(len(shape))])
    return level


def bell_draw(key, dims, spread, most, split=(), kind=jnp.bfloat16):
    drawn = spread * jax.random.normal(key, dims, jnp.float32)
    if split:
        drawn = drawn * shard_levels(key, dims, split, -0.22, 0.18)
    return jnp.clip(drawn, -most, most).astype(kind)


def setup_inputs(seed: int = 0) -> dict:
    splits = jax.random.split(jax.random.key(seed), 10)
    return {
        "queries": bell_draw(splits[0], (TOKENS, HEADS * HDIM), 0.022, 0.14941406, ((0, 32), (1, 4))),
        "key_rows": bell_draw(splits[1], (TOKENS, HEADS * HDIM), 0.022, 0.14941406, ((0, 32), (1, 4))),
        "value_rows": bell_draw(splits[2], (TOKENS, HEADS * HDIM), 0.022, 0.14941406, ((0, 32), (1, 4))),
        "grad_out": bell_draw(splits[3], (TOKENS, HEADS * HDIM), 1.0, 6.0, ((0, 32), (1, 4))),
        "accepted": plant((jax.random.randint(splits[4], (TOKENS,), 0, 4) < 3).astype(jnp.int32), jax.random.fold_in(splits[4], 1), 0, 1),
        "decay_code": plant(jax.random.randint(splits[5], (HEADS,), 14, 41), jax.random.fold_in(splits[5], 1), 14, 40).astype(jnp.int32),
        "w_query": bell_draw(splits[6], (D, HEADS * HDIM), D ** -0.5, 0.078125, ((1, 4),)),
        "w_key": bell_draw(splits[7], (D, HEADS * HDIM), D ** -0.5, 0.078125, ((1, 4),)),
        "w_value": bell_draw(splits[8], (D, HEADS * HDIM), D ** -0.5, 0.078125, ((1, 4),)),
    }


PRECISION_HIGH = lax.Precision.HIGHEST


def split_heads(array, heads, width, block):
    rows = array.shape[0]
    shaped = array.astype(jnp.float32).reshape(rows // block, block, heads, width)
    return shaped.transpose(0, 2, 1, 3)


def join_heads(array):
    count, heads, block, width = array.shape
    return array.transpose(0, 2, 1, 3).reshape(count * block, heads * width)


def decay_tables(rate, block):
    where_pos = jnp.arange(block, dtype=jnp.float32)
    diff = where_pos[:, None] - where_pos[None, :]
    inside = jnp.where(diff[None] >= 0, jnp.exp(-rate[:, None, None] * jnp.maximum(diff, 0.0)[None]), 0.0)
    leading_decay = jnp.exp(-rate[:, None] * (where_pos + 1.0)[None])
    segment_begin = jnp.exp(-rate[:, None] * where_pos[None])
    lag = jnp.exp(-rate[:, None] * (block - where_pos)[None])
    tail = jnp.exp(-rate[:, None] * (block - 1.0 - where_pos)[None])
    whole = jnp.exp(-rate * block)
    return inside, leading_decay, segment_begin, lag, tail, whole


def forward_sweep(qs, ks, vs, gs, tables, state_in):
    inside, leading_decay, segment_begin, lag, tail, whole = tables

    def step(running_state, parts):
        query_segment, kc, vc, gradient_segment = parts
        scores = jnp.einsum('hid,hjd->hij', gradient_segment, vc, precision=PRECISION_HIGH) * inside
        query_gradient = jnp.einsum('hij,hjd->hid', scores, kc, precision=PRECISION_HIGH)
        query_gradient = query_gradient + leading_decay[:, :, None] * jnp.einsum('pkv,pqv->pkq', gradient_segment, running_state, precision=PRECISION_HIGH)
        state_increment = jnp.einsum('hja,hjb->hab', kc * tail[:, :, None], vc, precision=PRECISION_HIGH)
        return whole[:, None, None] * running_state + state_increment, query_gradient

    final, query_gradient = lax.scan(step, state_in, (qs, ks, vs, gs))
    return query_gradient


def backward_sweep(qs, ks, vs, gs, tables, state_in):
    inside, leading_decay, segment_begin, lag, tail, whole = tables

    def step(running_state, parts):
        query_segment, kc, vc, gradient_segment = parts
        scores = jnp.einsum('hid,hjd->hij', gradient_segment, vc, precision=PRECISION_HIGH) * inside
        match = jnp.einsum('hid,hjd->hij', query_segment, kc, precision=PRECISION_HIGH) * inside
        grad_v = jnp.einsum('hij,hid->hjd', match, gradient_segment, precision=PRECISION_HIGH)
        grad_v = grad_v + lag[:, :, None] * jnp.einsum('hja,hab->hjb', kc, running_state, precision=PRECISION_HIGH)
        grad_k = jnp.einsum('hij,hid->hjd', scores, query_segment, precision=PRECISION_HIGH)
        grad_k = grad_k + lag[:, :, None] * jnp.einsum('hjb,hab->hja', vc, running_state, precision=PRECISION_HIGH)
        state_increment = jnp.einsum('rek,rem->rkm', query_segment * segment_begin[:, :, None], gradient_segment, precision=PRECISION_HIGH)
        return whole[:, None, None] * running_state + state_increment, (grad_k, grad_v)

    final, grads = lax.scan(step, state_in, (qs, ks, vs, gs), reverse=True)
    return grads


def reference(queries, key_rows, value_rows, grad_out, accepted, decay_code, w_query, w_key, w_value):
    rate = jnp.exp2(-0.5 * decay_code.astype(jnp.float32))
    masked = grad_out * accepted[:, None].astype(jnp.bfloat16)
    qs = split_heads(queries, HEADS, HDIM, GROUP)
    ks = split_heads(key_rows, HEADS, HDIM, GROUP)
    vs = split_heads(value_rows, HEADS, HDIM, GROUP)
    gs = split_heads(masked, HEADS, HDIM, GROUP)
    tables = decay_tables(rate, GROUP)
    empty = jnp.zeros((HEADS, HDIM, HDIM), jnp.float32)
    query_gradient = forward_sweep(qs, ks, vs, gs, tables, empty)
    grad_k, grad_v = backward_sweep(qs, ks, vs, gs, tables, empty)
    query_gradient = join_heads(query_gradient).astype(jnp.bfloat16)
    grad_k = join_heads(grad_k).astype(jnp.bfloat16)
    grad_v = join_heads(grad_v).astype(jnp.bfloat16)
    total = jnp.dot(query_gradient, w_query.T, preferred_element_type=jnp.float32)
    total = total + jnp.dot(grad_k, w_key.T, preferred_element_type=jnp.float32)
    total = total + jnp.dot(grad_v, w_value.T, preferred_element_type=jnp.float32)
    return total.astype(jnp.bfloat16)
```

```python
import jax
import jax.numpy as jnp
from jax import lax
from jax.experimental import pallas as pl
from jax.experimental.pallas import tpu as pltpu
from jax.sharding import PartitionSpec as P

BLK = 256
HDIM = 128
bf16 = jnp.bfloat16
f32 = jnp.float32
VMEM_LIMIT = 48 * 1024 * 1024

SEQ = 32


def place(z, x, c):
    return (z % 4) * 8 + (x % 4) * 2 + c % 2


CORE_SWAP = [(place(z, x, c), place(z, x, 1 - c)) for z in range(4) for x in range(4) for c in range(2)]
X_GROUPS = [[place(z, x, c) for x in range(4)] for z in range(4) for c in range(2)]
Z_GROUPS = [[place(z, x, c) for z in range(4)] for x in range(4) for c in range(2)]


def nt(a, b):
    return lax.dot_general(a, b, (((1,), (1,)), ((), ())), preferred_element_type=f32)


def nn(a, b):
    return lax.dot_general(a, b, (((1,), (0,)), ((), ())), preferred_element_type=f32)


def tn(a, b):
    return lax.dot_general(a, b, (((0,), (0,)), ((), ())), preferred_element_type=f32)


def spec(*shape):
    return jax.ShapeDtypeStruct(shape, bf16)


def params():
    return pltpu.CompilerParams(vmem_limit_bytes=VMEM_LIMIT)


def whole(count):
    return [pl.BlockSpec(memory_space=pltpu.VMEM)] * count


def stack_kernel(q, k, v, g, acc, first, second):
    rows = first.shape[0]
    width = q.shape[1]
    for half, out in enumerate((first, second)):
        at = pl.ds(half * rows, rows)
        out[:, 0:width] = q[at]
        out[:, width : 2 * width] = k[at]
        out[:, 2 * width : 3 * width] = v[at]
        keep = acc[0:1, half * rows : (half + 1) * rows].astype(f32)
        column = jnp.broadcast_to(keep, (HDIM, rows)).T
        wide = jnp.concatenate([column] * (width // HDIM), axis=1)
        out[:, 3 * width :] = (g[at].astype(f32) * wide).astype(bf16)


def stack(q, k, v, g, accepted):
    rows, width = q.shape
    return pl.pallas_call(
        stack_kernel,
        out_shape=[spec(rows // 2, 4 * width)] * 2,
        in_specs=whole(5),
        out_specs=whole(2),
        compiler_params=params(),
        cost_estimate=pl.CostEstimate(flops=0, bytes_accessed=16 * rows * width, transcendentals=0),
        name="stack",
    )(q, k, v, g, accepted.reshape(1, rows))


def sums_kernel(codes, first, second, out):
    rows = first.shape[0]
    heads = out.shape[2]
    width = heads * HDIM
    where = lax.broadcasted_iota(jnp.int32, (rows, HDIM), 0).astype(f32)
    for head in range(heads):
        rate = jnp.exp2(-0.5 * codes[head : head + 1, :].astype(f32))
        to_end = jnp.exp(-rate * (rows - 1.0 - where))
        from_start = jnp.exp(-rate * where)
        for half, raw in enumerate((first, second)):
            q, k, v, g = (raw[:, part * width + head * HDIM : part * width + (head + 1) * HDIM] for part in range(4))
            out[half, 0, head] = tn((k.astype(f32) * to_end).astype(bf16), v)
            out[half, 1, head] = tn((q.astype(f32) * from_start).astype(bf16), g)


def sums(codes, first, second, heads):
    return pl.pallas_call(
        sums_kernel,
        out_shape=jax.ShapeDtypeStruct((2, 2, heads, HDIM, HDIM), f32),
        in_specs=whole(3),
        out_specs=pl.BlockSpec(memory_space=pltpu.VMEM),
        compiler_params=params(),
        cost_estimate=pl.CostEstimate(flops=10**9, bytes_accessed=4 * 10**6, transcendentals=0),
        name="sums",
    )(codes, first, second)


def attend_kernel(upper, lower, state, out):
    heads = (state.shape[0] - 16) // (2 * HDIM)
    width = heads * HDIM
    row = lax.broadcasted_iota(jnp.int32, (BLK, BLK), 0)
    col = lax.broadcasted_iota(jnp.int32, (BLK, BLK), 1)
    below = row >= col
    above = col >= row
    row_pos = row.astype(f32)
    col_pos = col.astype(f32)
    where = lax.broadcasted_iota(jnp.int32, (BLK, HDIM), 0).astype(f32)
    for head in range(heads):
        code = state[2 * width + head : 2 * width + head + 1, :].astype(f32)
        rate1 = jnp.exp2(-0.5 * code)
        rate = jnp.concatenate([rate1, rate1], axis=1)
        inside = jnp.where(below, jnp.exp(-rate * jnp.maximum(row_pos - col_pos, 0.0)), 0.0)
        inside_t = jnp.where(above, jnp.exp(-rate * jnp.maximum(col_pos - row_pos, 0.0)), 0.0)
        across = jnp.exp(-rate * (BLK + row_pos - col_pos))
        across_t = jnp.exp(-rate * (BLK + col_pos - row_pos))
        lead = jnp.exp(-rate1 * (where + 1.0))
        lag = jnp.exp(-rate1 * (BLK - where))
        whole_block = jnp.exp(-rate1 * BLK)
        at = lambda raw, part: raw[:, part * width + head * HDIM : part * width + (head + 1) * HDIM]
        q0, k0, v0, g0 = (at(upper, part) for part in range(4))
        q1, k1, v1, g1 = (at(lower, part) for part in range(4))
        kv = state[head * HDIM : (head + 1) * HDIM, :]
        qg = state[width + head * HDIM : width + (head + 1) * HDIM, :]
        cut = lambda a, d: (a * d).astype(bf16)
        p00 = cut(nt(g0, v0), inside)
        p10 = cut(nt(g1, v0), across)
        p11 = cut(nt(g1, v1), inside)
        t00 = cut(nt(v0, g0), inside_t)
        t01 = cut(nt(v0, g1), across_t)
        t11 = cut(nt(v1, g1), inside_t)
        m00 = cut(nt(k0, q0), inside_t)
        m01 = cut(nt(k0, q1), across_t)
        m11 = cut(nt(k1, q1), inside_t)
        dq0 = nn(p00, k0) + lead * nt(g0, kv)
        dq1 = nn(p10, k0) + nn(p11, k1) + (lead * whole_block) * nt(g1, kv)
        dk0 = nn(t00, q0) + nn(t01, q1) + (lag * whole_block) * nt(v0, qg)
        dk1 = nn(t11, q1) + lag * nt(v1, qg)
        dv0 = nn(m00, g0) + nn(m01, g1) + (lag * whole_block) * nn(k0, qg)
        dv1 = nn(m11, g1) + lag * nn(k1, qg)
        for part, pair in enumerate(((dq0, dq1), (dk0, dk1), (dv0, dv1))):
            here = pl.ds(part * width + head * HDIM, HDIM)
            out[0:BLK, here] = pair[0].astype(bf16)
            out[BLK:, here] = pair[1].astype(bf16)


def attend(upper, lower, state):
    wide = upper.shape[1]
    return pl.pallas_call(
        attend_kernel,
        out_shape=spec(2 * BLK, wide // 4 * 3),
        in_specs=whole(3),
        out_specs=pl.BlockSpec(memory_space=pltpu.VMEM),
        compiler_params=params(),
        cost_estimate=pl.CostEstimate(flops=2 * 10**9, bytes_accessed=2 * 10**6, transcendentals=0),
        name="attend",
    )(upper, lower, state)


def pieces_kernel(at, a, b, c, out):
    width = a.shape[-1]
    for part, w in enumerate((a, b, c)):
        out[:, :, part * width : (part + 1) * width] = w[:, 0]


def pieces(at, weights, groups):
    rows, width = weights[0].shape
    share = rows // (groups * SEQ)
    shaped = [w.reshape(groups, SEQ, share, width) for w in weights]
    block = pl.BlockSpec((groups, 1, share, width), lambda i, at: (0, at[0], 0, 0))
    return pl.pallas_call(
        pieces_kernel,
        out_shape=spec(groups, share, 3 * width),
        grid_spec=pltpu.PrefetchScalarGridSpec(
            num_scalar_prefetch=1,
            grid=(1,),
            in_specs=[block] * 3,
            out_specs=pl.BlockSpec((groups, share, 3 * width), lambda i, at: (0, 0, 0)),
        ),
        compiler_params=params(),
        name="pieces",
    )(at, *shaped)


def project_kernel(order, g0, a0, b0, c0, g1, a1, b1, c10, c11, w, out):
    cols = out.shape[1]
    depth = g0.shape[1]
    load = lambda src: w[:, pl.ds(order[src], 1)].reshape(cols, depth)
    half = g0.shape[0]
    total = None
    for src, part in enumerate((g0, a0, b0, c0)):
        term = nt(part[...], load(src))
        total = term if total is None else total + term
    out[0:half] = total.astype(bf16)
    total = None
    for src, part in enumerate((g1, a1, b1)):
        term = nt(part[...], load(src))
        total = term if total is None else total + term
    last = load(3)
    quarter = half // 2
    out[half : half + quarter] = (total[0:quarter] + nt(c10[...], last)).astype(bf16)
    out[half + quarter :] = (total[quarter:] + nt(c11[...], last)).astype(bf16)


def project(order, parts, w):
    steps = 4
    rows = 2 * parts[0].shape[0]
    seq, groups, share, depth = w.shape
    cols = seq * share // steps
    full = lambda a: pl.BlockSpec(a.shape, lambda i, order: (0, 0))
    return pl.pallas_call(
        project_kernel,
        out_shape=spec(rows, seq * share),
        grid_spec=pltpu.PrefetchScalarGridSpec(
            num_scalar_prefetch=1,
            grid=(steps,),
            in_specs=[full(a) for a in parts]
            + [pl.BlockSpec((seq // steps, groups, share, depth), lambda i, order: (i, 0, 0, 0))],
            out_specs=pl.BlockSpec((rows, cols), lambda i, order: (0, i)),
        ),
        compiler_params=params(),
        cost_estimate=pl.CostEstimate(flops=10**10, bytes_accessed=19 * 10**6, transcendentals=0),
        name="project",
    )(order, *parts, w)


def turn(a, by):
    return lax.ppermute(a, "head", [(i, (i + by) % 4) for i in range(4)])


def ring(a):
    half = a.shape[0] // 2
    left = turn(a, 1)
    right = turn(a, -1)
    return left, right, turn(left[:half], 1), turn(right[half:], -1)


def powers(rate, span, counts):
    return jnp.exp(-rate * span * counts)


def enter(local, rate):
    seq = lax.axis_index("seq")
    z, x, c = seq // 8, (seq // 2) % 4, seq % 2
    late = (c == 1)
    rows = 1024.0
    r = rate[:, None, None]
    one = jnp.exp(-r * rows)
    two = jnp.exp(-r * (2 * rows))
    message = local.astype(bf16)
    other = lax.ppermute(message, "seq", CORE_SWAP).astype(f32)
    mine = message.astype(f32)
    first = jnp.where(late, other, mine)
    second = jnp.where(late, mine, other)
    chip = jnp.stack([one * first[0] + second[0], first[1] + one * second[1]]).astype(bf16)
    line = lax.all_to_all(
        jnp.broadcast_to(chip[None], (4, *chip.shape)), "seq", 0, 0, axis_index_groups=X_GROUPS
    ).astype(f32)
    there = jnp.arange(4)
    step = lambda gap, span: jnp.where(
        gap[:, None] >= 0, jnp.exp(-rate[None] * (span * jnp.maximum(gap, 0).astype(f32)[:, None])), 0.0
    )[:, :, None, None]
    span2, span8 = 2 * rows, 8 * rows
    before = (step(x - 1 - there, span2) * line[:, 0]).sum(0)
    after = (step(there - x - 1, span2) * line[:, 1]).sum(0)
    line_kv = (step(3 - there, span2) * line[:, 0]).sum(0)
    line_qg = (step(there, span2) * line[:, 1]).sum(0)
    up = (there > z)[:, None, None, None]
    send = jnp.where(up, line_kv[None], line_qg[None]).astype(bf16)
    column = lax.all_to_all(send, "seq", 0, 0, axis_index_groups=Z_GROUPS).astype(f32)
    far_kv = (step(z - 1 - there, span8) * column).sum(0)
    far_qg = (step(there - z - 1, span8) * column).sum(0)
    xf = x.astype(f32)
    kv = before + jnp.exp(-r * (span2 * xf)) * far_kv
    qg = after + jnp.exp(-r * (span2 * (3.0 - xf))) * far_qg
    kv = jnp.where(late, one * kv + other[0], kv)
    qg = jnp.where(late, qg, one * qg + other[1])
    return kv, qg


def shards(queries, key_rows, value_rows, grad_out, accepted, decay_code, w_query, w_key, w_value):
    heads = decay_code.shape[0]
    seq = lax.axis_index("seq").astype(jnp.int32)
    y = lax.axis_index("head").astype(jnp.int32)
    rate = jnp.exp2(-0.5 * decay_code.astype(f32))
    first, second = stack(queries, key_rows, value_rows, grad_out, accepted)
    a0, b0, c00, c01 = ring(first)

    own = pieces(seq.reshape(1), (w_query, w_key, w_value), 4)
    got = lax.all_to_all(own, "head", 0, 0)
    w = lax.all_gather(got, "seq")

    codes = jnp.broadcast_to(decay_code.astype(bf16)[:, None], (heads, HDIM))
    code_rows = jnp.pad(codes, ((0, 16 - heads), (0, 0)))
    local = sums(code_rows, first, second, heads)
    half = jnp.exp(-rate * first.shape[0])[:, None, None]
    kv_all = half * local[0, 0] + local[1, 0]
    qg_all = local[0, 1] + half * local[1, 1]
    kv_in, qg_in = enter(jnp.stack([kv_all, qg_all]), rate)
    kv_mid = half * kv_in + local[0, 0]
    qg_mid = half * qg_in + local[1, 1]

    def pack(kv, qg):
        return jnp.concatenate([kv.astype(bf16).reshape(-1, HDIM), qg.astype(bf16).reshape(-1, HDIM), code_rows], 0)

    state0 = pack(kv_in, qg_mid)
    state1 = pack(kv_mid, qg_in)
    states = lax.all_to_all(jnp.broadcast_to(state0[None], (4, *state0.shape)), "head", 0, 0)
    pick = lambda by: lax.dynamic_index_in_dim(states, (y + by) % 4, 0, False)

    done1 = attend(second[:BLK], second[BLK:], state1)
    a1, b1, c10, c11 = ring(done1)
    done0 = attend(first[:BLK], first[BLK:], state0)
    left0 = attend(a0[:BLK], a0[BLK:], pick(3))
    right0 = attend(b0[:BLK], b0[BLK:], pick(1))
    far0 = attend(c00, c01, pick(2))
    order = (y + jnp.array([0, 3, 1, 2], jnp.int32)) % 4
    return project(order, (done0, left0, right0, far0, done1, a1, b1, c10, c11), w)


def solution(mesh):
    in_specs = (P("seq", "head"),) * 4 + (P("seq"), P("head")) + (P(None, "head"),) * 3
    return jax.shard_map(shards, mesh=mesh, in_specs=in_specs, out_specs=P("seq", "head"), check_vma=False)
```

```python
import functools

import jax
import jax.numpy as jnp
from jax import lax
from jax.experimental import pallas as pl
from jax.experimental.pallas import tpu as pltpu
from jax.sharding import PartitionSpec as P

BLK = 256
EARLY = 512
HDIM = 128
bf16 = jnp.bfloat16
f32 = jnp.float32
VMEM_LIMIT = 24 * 1024 * 1024
VMEM_ALL = 62 * 1024 * 1024
LIGHT = pl.CostEstimate(flops=1, bytes_accessed=1, transcendentals=0)

SHARES = 8


def place(z, x, c):
    return (z % 4) * 8 + (x % 4) * 2 + c % 2


def nt(a, b):
    return lax.dot_general(a, b, (((1,), (1,)), ((), ())), preferred_element_type=f32)


def nn(a, b):
    return lax.dot_general(a, b, (((1,), (0,)), ((), ())), preferred_element_type=f32)


def tn(a, b):
    return lax.dot_general(a, b, (((0,), (0,)), ((), ())), preferred_element_type=f32)


def spec(*shape):
    return jax.ShapeDtypeStruct(shape, bf16)


def params():
    return pltpu.CompilerParams(vmem_limit_bytes=VMEM_LIMIT)


def whole(count):
    return [pl.BlockSpec(memory_space=pltpu.VMEM)] * count


def fetch(pairs, sems):
    copies = [pltpu.make_async_copy(source, target, sems.at[i]) for i, (source, target) in enumerate(pairs)]
    for copy in copies:
        copy.start()
    return copies


def begin_kernel(
    q, k, v, g, accepted, decay_code, wq, wk, wv, first, second, codes, local, message, s1, s2, s3, raw_g, keep, sems
):
    width = q.shape[1]
    cut = first.shape[0]
    parts = ((0, cut, first), (cut, second.shape[0], second))
    pairs = [(g, raw_g), (accepted, keep)]
    for part, ref in enumerate((q, k, v)):
        for start, rows, out in parts:
            pairs.append((ref.at[pl.ds(start, rows)], out.at[:, pl.ds(part * width, width)]))
    y = lax.axis_index("head")
    z, x, c = spot()
    piece = c * 4 + jnp.where(c == 0, z, x)
    for out, by in zip((s1, s2, s3), (1, 3, 2)):
        for part, w in enumerate((wq, wk, wv)):
            pairs.append((w.at[lax.rem(y + by, 4), piece], out.at[:, pl.ds(part * width, width)]))
    copies = fetch(pairs, sems)
    line = lax.broadcasted_iota(jnp.int32, codes.shape, 0)
    filled = jnp.zeros(codes.shape, f32)
    for head in range(decay_code.shape[0]):
        filled = jnp.where(line == head, decay_code[head].astype(f32), filled)
    codes[...] = filled.astype(bf16)
    for copy in copies[:2]:
        copy.wait()
    for start, rows, out in parts:
        column = jnp.broadcast_to(keep[0:1, start : start + rows].astype(f32), (HDIM, rows)).T
        wide = jnp.concatenate([column] * (width // HDIM), axis=1)
        out[:, 3 * width :] = (raw_g[start : start + rows].astype(f32) * wide).astype(bf16)
    for copy in copies[2:]:
        copy.wait()
    for head in range(local.shape[2]):
        rate = jnp.exp2(-0.5 * jnp.full((1, HDIM), decay_code[head], f32))
        found, spans = [], []
        for half, (begin_row, end_row) in enumerate(((0, cut), (cut, q.shape[0]))):
            spans.append(jnp.exp(-rate * (end_row - begin_row)))
            kv = qg = jnp.zeros((HDIM, HDIM), f32)
            for start, rows, raw in parts:
                if begin_row <= start < end_row:
                    where = lax.broadcasted_iota(jnp.int32, (rows, HDIM), 0).astype(f32) + (start - begin_row)
                    to_end = jnp.exp(-rate * (end_row - begin_row - 1.0 - where))
                    from_start = jnp.exp(-rate * where)
                    at = lambda part: raw[:, part * width + head * HDIM : part * width + (head + 1) * HDIM]
                    kv += tn((at(1).astype(f32) * to_end).astype(bf16), at(2))
                    qg += tn((at(0).astype(f32) * from_start).astype(bf16), at(3))
            found.append((kv, qg))
            local[half, 0, head] = kv
            local[half, 1, head] = qg
        message[0, head] = (spans[1] * found[0][0] + found[1][0]).astype(bf16)
        message[1, head] = (found[0][1] + spans[0] * found[1][1]).astype(bf16)


def begin(q, k, v, g, accepted, decay_code, weights, early):
    rows, width = q.shape
    out_rows = weights[0].shape[0]
    share = out_rows // (4 * SHARES)
    shaped = [w.reshape(4, SHARES, share, width) for w in weights]
    heads = decay_code.shape[0]
    far = pl.BlockSpec(memory_space=pl.ANY)
    return pl.pallas_call(
        begin_kernel,
        out_shape=[
            spec(early, 4 * width),
            spec(rows - early, 4 * width),
            spec(16, HDIM),
            jax.ShapeDtypeStruct((2, 2, heads, HDIM, HDIM), f32),
            spec(2, heads, HDIM, HDIM),
            *[spec(share, 3 * width)] * 3,
        ],
        in_specs=[far] * 5 + [pl.BlockSpec(memory_space=pltpu.SMEM)] + [far] * 3,
        out_specs=whole(8),
        scratch_shapes=[
            pltpu.VMEM((rows, width), bf16),
            pltpu.VMEM((1, rows), jnp.int32),
            pltpu.SemaphoreType.DMA((17,)),
        ],
        compiler_params=pltpu.CompilerParams(vmem_limit_bytes=VMEM_ALL),
        cost_estimate=LIGHT,
        name="begin",
    )(q, k, v, g, accepted.reshape(1, rows), decay_code, *shaped)


def spot():
    seq = lax.axis_index("seq")
    return lax.div(seq, 8), lax.rem(lax.div(seq, 2), 4), lax.rem(seq, 2)


def fade(codes, head, span, count):
    rate = jnp.exp2(-0.5 * codes[head : head + 1, :].astype(f32))
    faded = jnp.exp(-rate * (span * jnp.maximum(count, 0).astype(f32)))
    return jnp.where(count >= 0, faded, 0.0)


def join_kernel(rows, codes_at, mine_at, other_at, out, codes, mine, other, sems):
    z, x, c = spot()
    late = c == 1
    chip = z * 4 + x
    for copy in fetch([(codes_at, codes), (mine_at, mine), (other_at, other)], sems):
        copy.wait()
    for head in range(mine.shape[1]):
        one = fade(codes, head, rows, jnp.int32(1))
        near, far = mine[:, head].astype(f32), other[:, head].astype(f32)
        before, after = jnp.where(late, far, near), jnp.where(late, near, far)
        kv = (one * before[0] + after[0]).astype(bf16)
        qg = (before[1] + one * after[1]).astype(bf16)
        for to in range(out.shape[0]):
            out[to, head] = jnp.where(to > chip, kv, qg)


def join(rows, codes, mine, other):
    return pl.pallas_call(
        functools.partial(join_kernel, rows),
        out_shape=spec(16, *mine.shape[1:]),
        in_specs=[pl.BlockSpec(memory_space=pl.ANY)] * 3,
        out_specs=pl.BlockSpec(memory_space=pltpu.VMEM),
        scratch_shapes=[
            pltpu.VMEM(codes.shape, bf16),
            pltpu.VMEM(mine.shape, bf16),
            pltpu.VMEM(other.shape, bf16),
            pltpu.SemaphoreType.DMA((3,)),
        ],
        compiler_params=pltpu.CompilerParams(vmem_limit_bytes=VMEM_ALL),
        cost_estimate=LIGHT,
        name="join",
    )(codes, mine, other)


def enter_kernel(early, rows, codes, arrived, other, local, state0, state1):
    z, x, c = spot()
    late = c == 1
    chip = z * 4 + x
    heads = arrived.shape[1]
    width = heads * HDIM
    for head in range(heads):
        kv = qg = jnp.zeros((HDIM, HDIM), f32)
        for there in range(arrived.shape[0]):
            it = arrived[there, head].astype(f32)
            kv += it * fade(codes, head, 2 * rows, chip - 1 - there)
            qg += it * fade(codes, head, 2 * rows, there - chip - 1)
        one = fade(codes, head, rows, jnp.int32(1))
        start = fade(codes, head, early, jnp.int32(1))
        end = fade(codes, head, rows - early, jnp.int32(1))
        kv = jnp.where(late, one * kv + other[0, head].astype(f32), kv)
        qg = jnp.where(late, qg, one * qg + other[1, head].astype(f32))
        here = pl.ds(head * HDIM, HDIM)
        there = pl.ds(width + head * HDIM, HDIM)
        state0[here] = kv.astype(bf16)
        state0[there] = (end * qg + local[1, 1, head]).astype(bf16)
        state1[here] = (start * kv + local[0, 0, head]).astype(bf16)
        state1[there] = qg.astype(bf16)
    state0[2 * width :] = codes[...]
    state1[2 * width :] = codes[...]


def small(kernel, rows, operands, outs, name):
    return pl.pallas_call(
        functools.partial(kernel, rows),
        out_shape=outs,
        in_specs=whole(len(operands)),
        out_specs=whole(len(outs)),
        compiler_params=params(),
        cost_estimate=LIGHT,
        name=name,
    )(*operands)


def attend_rows(raws, state, out):
    heads = (state.shape[0] - 16) // (2 * HDIM)
    width = heads * HDIM
    rows = out.shape[0]
    starts = list(range(0, rows, BLK))
    sizes = [min(BLK, rows - start) for start in starts]
    count = len(starts)
    edges = [0]
    for raw in raws:
        edges.append(edges[-1] + raw.shape[0])

    def take(block, part, head):
        low, high = starts[block], starts[block] + sizes[block]
        here = slice(part * width + head * HDIM, part * width + (head + 1) * HDIM)
        found = []
        for raw, start, end in zip(raws, edges, edges[1:]):
            if max(low, start) < min(high, end):
                found.append(raw[max(low, start) - start : min(high, end) - start, here])
        return found[0] if len(found) == 1 else jnp.concatenate(found, axis=0)

    def table(rate1, later, earlier, flip):
        shape = (sizes[earlier], sizes[later]) if flip else (sizes[later], sizes[earlier])
        row = lax.broadcasted_iota(jnp.int32, shape, 0)
        col = lax.broadcasted_iota(jnp.int32, shape, 1)
        rate = rate1 if shape[1] == HDIM else jnp.concatenate([rate1] * (shape[1] // HDIM), axis=1)
        gap = (col - row if flip else row - col).astype(f32)
        if later == earlier:
            return jnp.where(gap >= 0, jnp.exp(-rate * jnp.maximum(gap, 0.0)), 0.0)
        return jnp.exp(-rate * (starts[later] - starts[earlier] + gap))

    cut = lambda a, d: (a * d).astype(bf16)
    for head in range(heads):
        code = state[2 * width + head : 2 * width + head + 1, :].astype(f32)
        rate = jnp.exp2(-0.5 * code)
        made = {}

        def decay(later, earlier, flip):
            key = (starts[later] - starts[earlier], sizes[later], sizes[earlier], flip)
            if key not in made:
                made[key] = table(rate, later, earlier, flip)
            return made[key]

        q, k, v, g = ([take(block, part, head) for block in range(count)] for part in range(4))
        kv = state[head * HDIM : (head + 1) * HDIM, :]
        qg = state[width + head * HDIM : width + (head + 1) * HDIM, :]
        for block in range(count):
            start, size = starts[block], sizes[block]
            where = lax.broadcasted_iota(jnp.int32, (size, HDIM), 0).astype(f32) + start
            lag = jnp.exp(-rate * (rows - where))
            dq = jnp.exp(-rate * (where + 1.0)) * nt(g[block], kv)
            dk = lag * nt(v[block], qg)
            dv = lag * nn(k[block], qg)
            for other in range(block + 1):
                dq += nn(cut(nt(g[block], v[other]), decay(block, other, False)), k[other])
            for other in range(block, count):
                dk += nn(cut(nt(v[block], g[other]), decay(other, block, True)), q[other])
                dv += nn(cut(nt(k[block], q[other]), decay(other, block, True)), g[other])
            for part, value in enumerate((dq, dk, dv)):
                here = pl.ds(part * width + head * HDIM, HDIM)
                out[start : start + size, here] = value.astype(bf16)


def attend_both(first, second, state0, state1, upper, lower):
    attend_rows([first], state0, upper)
    attend_rows([second], state1, lower)


def attend(first, second, state0, state1):
    depth = first.shape[1] // 4 * 3
    return pl.pallas_call(
        attend_both,
        out_shape=[spec(first.shape[0], depth), spec(second.shape[0], depth)],
        in_specs=whole(4),
        out_specs=whole(2),
        compiler_params=params(),
        cost_estimate=LIGHT,
        name="attend",
    )(first, second, state0, state1)


OWN_STEPS = 4


def own_kernel(upper, lower, wq, wk, wv, out, w, sems):
    y = lax.axis_index("head")
    cols, width = w.shape[1:]
    part = cols // OWN_STEPS
    pairs = []
    for step in range(OWN_STEPS):
        begins = pl.multiple_of(y * cols + step * part, part)
        pairs += [(ref.at[pl.ds(begins, part)], w.at[i, pl.ds(step * part, part)]) for i, ref in enumerate((wq, wk, wv))]
    copies = fetch(pairs, sems)
    cut = upper.shape[0]
    for step in range(OWN_STEPS):
        for copy in copies[3 * step : 3 * step + 3]:
            copy.wait()
        here = slice(step * part, (step + 1) * part)
        for rows, ref in ((slice(0, cut), upper), (slice(cut, None), lower)):
            total = None
            for i in range(3):
                term = nt(ref[:, i * width : (i + 1) * width], w[i, here])
                total = term if total is None else total + term
            out[rows, here] = total.astype(bf16)


def project_own(upper, lower, weights):
    rows = upper.shape[0] + lower.shape[0]
    cols, width = weights[0].shape[0] // 4, weights[0].shape[1]
    return pl.pallas_call(
        own_kernel,
        out_shape=spec(rows, cols),
        in_specs=whole(2) + [pl.BlockSpec(memory_space=pl.ANY)] * 3,
        out_specs=pl.BlockSpec(memory_space=pltpu.VMEM),
        scratch_shapes=[pltpu.VMEM((3, cols, width), bf16), pltpu.SemaphoreType.DMA((3 * OWN_STEPS,))],
        compiler_params=params(),
        cost_estimate=LIGHT,
        name="project_own",
    )(upper, lower, *weights)


def others_kernel(srcs, cores, last, *refs):
    refs = list(refs)
    take = lambda count: [refs.pop(0) for _ in range(count)]
    parts = [take(2) for _ in srcs]
    tables = take(len(cores))
    partial, out, w = take(3)
    z, x, c = spot()
    pieces, _, share, depth = tables[0].shape
    half = pieces * share
    tile = w.shape[1]
    made = []
    for table, mirrored in zip(tables, cores):
        core = 1 - c if mirrored else c
        outer = jnp.where(core == 0, z, x)
        for step in range(half // tile):
            at = pl.ds(pl.multiple_of(core * half + step * tile, tile), tile)
            for piece in range(tile // share):
                source = lax.rem(outer + 4 - (step * (tile // share) + piece), 4)
                for i, src in enumerate(srcs):
                    w[i, piece * share : (piece + 1) * share] = table[source, src - 1]
            start = 0
            for chunk in range(2):
                size = parts[0][chunk].shape[0]
                total = partial[start : start + size, at].astype(f32)
                for i in range(len(srcs)):
                    total = total + nt(parts[i][chunk][...], w[i])
                if last:
                    tiles, sems = refs
                    slot = len(made)
                    tiles[slot] = total.astype(bf16)
                    target = out.at[pl.ds(start, size), at]
                    made.append(pltpu.make_async_copy(tiles.at[slot], target, sems.at[slot]))
                    made[-1].start()
                else:
                    out[start : start + size, at] = total.astype(bf16)
                start += size
    for copy in made:
        copy.wait()


def project_others(srcs, parts, tables, mirrored, partial, last=False):
    rows, cols = partial.shape
    pieces, _, share, depth = tables[0].shape
    tile = 2 * share
    count = 2 * len(tables) * pieces * share // tile
    operands = [*sum(parts, []), *tables, partial]
    scratch = [pltpu.VMEM((len(srcs), tile, depth), bf16)]
    if last:
        scratch += [pltpu.VMEM((count, rows // 2, tile), bf16), pltpu.SemaphoreType.DMA((count,))]
    return pl.pallas_call(
        functools.partial(others_kernel, srcs, mirrored, last),
        out_shape=spec(rows, cols),
        in_specs=whole(len(operands)),
        out_specs=pl.BlockSpec(memory_space=pl.ANY if last else pltpu.VMEM),
        scratch_shapes=scratch,
        input_output_aliases={} if last else {len(operands) - 1: 0},
        compiler_params=params(),
        cost_estimate=LIGHT,
        name="project_others",
    )(*operands)


def turn(a, by):
    return lax.ppermute(a, "head", [(i, (i + by) % 4) for i in range(4)])


def move(a, where):
    pairs = [(place(z, x, c), place(*where(z, x, c))) for z in range(4) for x in range(4) for c in range(2)]
    return lax.ppermute(a, "seq", pairs)


def across(a):
    return move(a, lambda z, x, c: (z, x, 1 - c))


CHIPS = [[place(z, x, c) for z in range(4) for x in range(4)] for c in range(2)]
def major(a, by):
    return move(a, lambda z, x, c: (z + by, x, c) if c == 0 else (z, x + by, c))


def tie(*groups):
    return lax.optimization_barrier(groups)


def shards(queries, key_rows, value_rows, grad_out, accepted, decay_code, w_query, w_key, w_value):
    heads = decay_code.shape[0]
    count = queries.shape[0]
    rows = float(count)
    weights = (w_query, w_key, w_value)
    first, second, codes, local, message, *sent = begin(
        queries, key_rows, value_rows, grad_out, accepted, decay_code, weights, EARLY
    )
    other = across(message)
    leaving = join(rows, codes, message, other)
    share = jnp.stack([turn(sent[0], 1), turn(sent[1], -1), turn(sent[2], 2)])
    arrived = lax.all_to_all(leaving, "seq", 0, 0, axis_index_groups=CHIPS)
    share, _ = tie(share, leaving)
    half = [share] + [major(share, by) for by in (1, 2, 3)]
    state0, state1 = small(
        functools.partial(enter_kernel, float(EARLY)),
        rows,
        (codes, arrived, other, local),
        [spec(2 * heads * HDIM + 16, HDIM)] * 2,
        "enter",
    )
    upper, lower = attend(first, second, state0, state1)
    upper_left, lower_right = turn(upper, 1), turn(lower, -1)
    lower_left, upper_right = turn(lower, 1), turn(upper, -1)
    upper_far, lower_far = turn(upper_left, 1), turn(lower_right, -1)
    half, _, _ = tie(half, upper_left, lower_right)
    half = jnp.stack(half)
    other_half = across(half)
    total = project_own(upper, lower, weights)
    sides = [upper_left, lower_left], [upper_right, lower_right]
    total = project_others((1, 2), sides, (half,), (False,), total)
    total = project_others((1, 2), sides, (other_half,), (True,), total)
    return project_others((3,), ([upper_far, lower_far],), (half, other_half), (False, True), total, True)


def solution(mesh):
    in_specs = (P("seq", "head"),) * 4 + (P("seq"), P("head")) + (P(None, "head"),) * 3
    return jax.shard_map(shards, mesh=mesh, in_specs=in_specs, out_specs=P("seq", "head"), check_vma=False)
```

```python
import functools

import jax
import jax.numpy as jnp
from jax import lax
from jax.experimental import pallas as pl
from jax.experimental.pallas import tpu as pltpu
from jax.sharding import PartitionSpec as P

BLK = 256
EARLY = 512
CHUNK = 256
HDIM = 128
bf16 = jnp.bfloat16
f32 = jnp.float32
VMEM_LIMIT = 24 * 1024 * 1024
VMEM_ALL = 62 * 1024 * 1024
LIGHT = pl.CostEstimate(flops=1, bytes_accessed=1, transcendentals=0)

SHARES = 8


def place(z, x, c):
    return (z % 4) * 8 + (x % 4) * 2 + c % 2


def nt(a, b):
    return lax.dot_general(a, b, (((1,), (1,)), ((), ())), preferred_element_type=f32)


def nn(a, b):
    return lax.dot_general(a, b, (((1,), (0,)), ((), ())), preferred_element_type=f32)


def tn(a, b):
    return lax.dot_general(a, b, (((0,), (0,)), ((), ())), preferred_element_type=f32)


def spec(*shape):
    return jax.ShapeDtypeStruct(shape, bf16)


def params():
    return pltpu.CompilerParams(vmem_limit_bytes=VMEM_LIMIT)


def whole(count):
    return [pl.BlockSpec(memory_space=pltpu.VMEM)] * count


def fetch(pairs, sems):
    copies = [pltpu.make_async_copy(source, target, sems.at[i]) for i, (source, target) in enumerate(pairs)]
    for copy in copies:
        copy.start()
    return copies


def begin_kernel(
    cut, q, k, v, g, accepted, decay_code, wq, wk, wv, raw, codes, local, message, s1, s2, s3, raw_g, keep, sems
):
    width = q.shape[1]
    rows = raw.shape[0]
    pairs = [(g, raw_g), (accepted, keep)]
    for part, ref in enumerate((q, k, v)):
        pairs.append((ref, raw.at[:, pl.ds(part * width, width)]))
    y = lax.axis_index("head")
    z, x, c = spot()
    piece = c * 4 + jnp.where(c == 0, z, x)
    for out, by in zip((s1, s2, s3), (1, 3, 2)):
        for part, w in enumerate((wq, wk, wv)):
            pairs.append((w.at[lax.rem(y + by, 4), piece], out.at[:, pl.ds(part * width, width)]))
    copies = fetch(pairs, sems)
    line = lax.broadcasted_iota(jnp.int32, codes.shape, 0)
    filled = jnp.zeros(codes.shape, f32)
    for head in range(decay_code.shape[0]):
        filled = jnp.where(line == head, decay_code[head].astype(f32), filled)
    codes[...] = filled.astype(bf16)
    for copy in copies[:2]:
        copy.wait()
    column = jnp.broadcast_to(keep[0:1, :].astype(f32), (HDIM, rows)).T
    wide = jnp.concatenate([column] * (width // HDIM), axis=1)
    raw[:, 3 * width :] = (raw_g[...].astype(f32) * wide).astype(bf16)
    for copy in copies[2:]:
        copy.wait()
    for head in range(local.shape[2]):
        rate = jnp.exp2(-0.5 * jnp.full((1, HDIM), decay_code[head], f32))
        found, spans = [], []
        for half, (low, high) in enumerate(((0, cut), (cut, rows))):
            where = lax.broadcasted_iota(jnp.int32, (high - low, HDIM), 0).astype(f32)
            to_end = jnp.exp(-rate * (high - low - 1.0 - where))
            from_start = jnp.exp(-rate * where)
            spans.append(jnp.exp(-rate * (high - low)))
            at = lambda part: raw[low:high, part * width + head * HDIM : part * width + (head + 1) * HDIM]
            kv = tn((at(1).astype(f32) * to_end).astype(bf16), at(2))
            qg = tn((at(0).astype(f32) * from_start).astype(bf16), at(3))
            found.append((kv, qg))
            local[half, 0, head] = kv
            local[half, 1, head] = qg
        message[0, head] = (spans[1] * found[0][0] + found[1][0]).astype(bf16)
        message[1, head] = (found[0][1] + spans[0] * found[1][1]).astype(bf16)


def begin(q, k, v, g, accepted, decay_code, weights, early):
    rows, width = q.shape
    out_rows = weights[0].shape[0]
    share = out_rows // (4 * SHARES)
    shaped = [w.reshape(4, SHARES, share, width) for w in weights]
    heads = decay_code.shape[0]
    far = pl.BlockSpec(memory_space=pl.ANY)
    return pl.pallas_call(
        functools.partial(begin_kernel, early),
        out_shape=[
            spec(rows, 4 * width),
            spec(16, HDIM),
            jax.ShapeDtypeStruct((2, 2, heads, HDIM, HDIM), f32),
            spec(2, heads, HDIM, HDIM),
            *[spec(share, 3 * width)] * 3,
        ],
        in_specs=[far] * 5 + [pl.BlockSpec(memory_space=pltpu.SMEM)] + [far] * 3,
        out_specs=whole(7),
        scratch_shapes=[
            pltpu.VMEM((rows, width), bf16),
            pltpu.VMEM((1, rows), jnp.int32),
            pltpu.SemaphoreType.DMA((14,)),
        ],
        compiler_params=pltpu.CompilerParams(vmem_limit_bytes=VMEM_ALL),
        cost_estimate=LIGHT,
        name="begin",
    )(q, k, v, g, accepted.reshape(1, rows), decay_code, *shaped)


def spot():
    seq = lax.axis_index("seq")
    return lax.div(seq, 8), lax.rem(lax.div(seq, 2), 4), lax.rem(seq, 2)


def fade(codes, head, span, count):
    rate = jnp.exp2(-0.5 * codes[head : head + 1, :].astype(f32))
    faded = jnp.exp(-rate * (span * jnp.maximum(count, 0).astype(f32)))
    return jnp.where(count >= 0, faded, 0.0)


def join_kernel(rows, codes_at, mine_at, other_at, out, codes, mine, other, sems):
    z, x, c = spot()
    late = c == 1
    chip = z * 4 + x
    for copy in fetch([(codes_at, codes), (mine_at, mine), (other_at, other)], sems):
        copy.wait()
    for head in range(mine.shape[1]):
        one = fade(codes, head, rows, jnp.int32(1))
        near, far = mine[:, head].astype(f32), other[:, head].astype(f32)
        before, after = jnp.where(late, far, near), jnp.where(late, near, far)
        kv = (one * before[0] + after[0]).astype(bf16)
        qg = (before[1] + one * after[1]).astype(bf16)
        for to in range(out.shape[0]):

            @pl.when(c == head)
            def _(to=to, kv=kv, qg=qg):
                out[to, 0] = jnp.where(to > chip, kv, qg)


def join(rows, codes, mine, other):
    return pl.pallas_call(
        functools.partial(join_kernel, rows),
        out_shape=spec(16, 1, *mine.shape[2:]),
        in_specs=[pl.BlockSpec(memory_space=pl.ANY)] * 3,
        out_specs=pl.BlockSpec(memory_space=pltpu.VMEM),
        scratch_shapes=[
            pltpu.VMEM(codes.shape, bf16),
            pltpu.VMEM(mine.shape, bf16),
            pltpu.VMEM(other.shape, bf16),
            pltpu.SemaphoreType.DMA((3,)),
        ],
        compiler_params=pltpu.CompilerParams(vmem_limit_bytes=VMEM_ALL),
        cost_estimate=LIGHT,
        name="join",
    )(codes, mine, other)


def gather_kernel(rows, decay_code, arrived, out):
    z, x, c = spot()
    chip = z * 4 + x
    kv = qg = jnp.zeros((HDIM, HDIM), f32)
    code = jnp.full((1, HDIM), jnp.where(c == 0, decay_code[0], decay_code[1]), jnp.int32)
    for there in range(arrived.shape[0]):
        it = arrived[there, 0].astype(f32)
        kv += it * fade(code, 0, 2 * rows, chip - 1 - there)
        qg += it * fade(code, 0, 2 * rows, there - chip - 1)
    out[0] = kv.astype(bf16)
    out[1] = qg.astype(bf16)


def enter_states(early, rows, codes, mine, theirs, other, local, state0, state1):
    z, x, c = spot()
    late = c == 1
    heads = other.shape[1]
    width = heads * HDIM
    for head in range(heads):
        kv = jnp.where(c == head, mine[0], theirs[0]).astype(f32)
        qg = jnp.where(c == head, mine[1], theirs[1]).astype(f32)
        one = fade(codes, head, rows, jnp.int32(1))
        start = fade(codes, head, early, jnp.int32(1))
        end = fade(codes, head, rows - early, jnp.int32(1))
        kv = jnp.where(late, one * kv + other[0, head].astype(f32), kv)
        qg = jnp.where(late, qg, one * qg + other[1, head].astype(f32))
        here = pl.ds(head * HDIM, HDIM)
        there = pl.ds(width + head * HDIM, HDIM)
        state0[here] = kv.astype(bf16)
        state0[there] = (end * qg + local[1, 1, head]).astype(bf16)
        state1[here] = (start * kv + local[0, 0, head]).astype(bf16)
        state1[there] = qg.astype(bf16)
    state0[2 * width :] = codes[...]
    state1[2 * width :] = codes[...]


def gather(rows, decay_code, arrived):
    return pl.pallas_call(
        functools.partial(gather_kernel, rows),
        out_shape=spec(2, HDIM, HDIM),
        in_specs=[pl.BlockSpec(memory_space=pltpu.SMEM), pl.BlockSpec(memory_space=pltpu.VMEM)],
        out_specs=pl.BlockSpec(memory_space=pltpu.VMEM),
        compiler_params=params(),
        cost_estimate=LIGHT,
        name="gather",
    )(decay_code, arrived)


def attend_rows(raws, state, out_rows, first_row, targets):
    heads = (state.shape[0] - 16) // (2 * HDIM)
    width = heads * HDIM
    rows = out_rows
    starts = list(range(0, rows, BLK))
    sizes = [min(BLK, rows - start) for start in starts]
    count = len(starts)
    edges = [0]
    for raw in raws:
        edges.append(edges[-1] + raw.shape[0])

    def take(block, part, head):
        low, high = starts[block], starts[block] + sizes[block]
        here = slice(part * width + head * HDIM, part * width + (head + 1) * HDIM)
        found = []
        for raw, start, end in zip(raws, edges, edges[1:]):
            if max(low, start) < min(high, end):
                found.append(raw[max(low, start) - start : min(high, end) - start, here])
        return found[0] if len(found) == 1 else jnp.concatenate(found, axis=0)

    def table(rate1, later, earlier, flip):
        shape = (sizes[earlier], sizes[later]) if flip else (sizes[later], sizes[earlier])
        row = lax.broadcasted_iota(jnp.int32, shape, 0)
        col = lax.broadcasted_iota(jnp.int32, shape, 1)
        rate = rate1 if shape[1] == HDIM else jnp.concatenate([rate1] * (shape[1] // HDIM), axis=1)
        gap = (col - row if flip else row - col).astype(f32)
        if later == earlier:
            return jnp.where(gap >= 0, jnp.exp(-rate * jnp.maximum(gap, 0.0)), 0.0)
        return jnp.exp(-rate * (starts[later] - starts[earlier] + gap))

    cut = lambda a, d: (a * d).astype(bf16)
    for head in range(heads):
        code = state[2 * width + head : 2 * width + head + 1, :].astype(f32)
        rate = jnp.exp2(-0.5 * code)
        made = {}

        def decay(later, earlier, flip):
            key = (starts[later] - starts[earlier], sizes[later], sizes[earlier], flip)
            if key not in made:
                made[key] = table(rate, later, earlier, flip)
            return made[key]

        q, k, v, g = ([take(block, part, head) for block in range(count)] for part in range(4))
        kv = state[head * HDIM : (head + 1) * HDIM, :]
        qg = state[width + head * HDIM : width + (head + 1) * HDIM, :]
        for block in range(count):
            start, size = starts[block], sizes[block]
            where = lax.broadcasted_iota(jnp.int32, (size, HDIM), 0).astype(f32) + start
            lag = jnp.exp(-rate * (rows - where))
            dq = jnp.exp(-rate * (where + 1.0)) * nt(g[block], kv)
            dk = lag * nt(v[block], qg)
            dv = lag * nn(k[block], qg)
            for other in range(block + 1):
                dq += nn(cut(nt(g[block], v[other]), decay(block, other, False)), k[other])
            for other in range(block, count):
                dk += nn(cut(nt(v[block], g[other]), decay(other, block, True)), q[other])
                dv += nn(cut(nt(k[block], q[other]), decay(other, block, True)), g[other])
            for part, value in enumerate((dq, dk, dv)):
                here = pl.ds(part * width + head * HDIM, HDIM)
                value = value.astype(bf16)
                low = first_row + start
                for ref, begins in targets:
                    from_row, to_row = max(low, begins), min(low + size, begins + ref.shape[0])
                    if from_row < to_row:
                        ref[from_row - begins : to_row - begins, here] = value[from_row - low : to_row - low]


def attend_kernel(early, rows, *refs):
    inputs, out, rest = refs[:6], refs[6], refs[7:]
    held, (state0, state1, made, sems, out_sems) = rest[:6], rest[6:]
    copies = fetch(list(zip(inputs, held)), sems)
    for copy in copies[:5]:
        copy.wait()
    count = made.shape[0]
    enter_states(float(early), rows, *held[:5], state0, state1)
    written = []

    def leave(low, high):
        written.append(pltpu.make_async_copy(made.at[low:high], out.at[low:high], out_sems.at[len(written)]))
        written[-1].start()

    copies[5].wait()
    attend_rows([held[5].at[0:early]], state0, early, 0, [(made, 0)])
    leave(0, early)
    attend_rows([held[5].at[early:]], state1, count - early, early, [(made, 0)])
    leave(early, count)
    for copy in written:
        copy.wait()


def attend(early, rows, codes, mine, theirs, other, local, raw):
    operands = (codes, mine, theirs, other, local, raw)
    count, depth = raw.shape[0], raw.shape[1] // 4 * 3
    state = pltpu.VMEM((2 * other.shape[1] * HDIM + codes.shape[0], HDIM), bf16)
    anywhere = pl.BlockSpec(memory_space=pl.ANY)
    return pl.pallas_call(
        functools.partial(attend_kernel, early, rows),
        out_shape=spec(count, depth),
        in_specs=[anywhere] * 6,
        out_specs=anywhere,
        scratch_shapes=[pltpu.VMEM(a.shape, a.dtype) for a in operands]
        + [state, state, pltpu.VMEM((count, depth), bf16)]
        + [pltpu.SemaphoreType.DMA((6,)), pltpu.SemaphoreType.DMA((2,))],
        compiler_params=pltpu.CompilerParams(vmem_limit_bytes=VMEM_ALL),
        cost_estimate=LIGHT,
        name="attend",
    )(*operands)


OWN_STEPS = 4


def own_kernel(done, wq, wk, wv, out, w, sems):
    y = lax.axis_index("head")
    cols, width = w.shape[1:]
    part = cols // OWN_STEPS
    pairs = []
    for step in range(OWN_STEPS):
        begins = pl.multiple_of(y * cols + step * part, part)
        pairs += [(ref.at[pl.ds(begins, part)], w.at[i, pl.ds(step * part, part)]) for i, ref in enumerate((wq, wk, wv))]
    copies = fetch(pairs, sems)
    for step in range(OWN_STEPS):
        for copy in copies[3 * step : 3 * step + 3]:
            copy.wait()
        here = slice(step * part, (step + 1) * part)
        total = None
        for i in range(3):
            term = nt(done[:, i * width : (i + 1) * width], w[i, here])
            total = term if total is None else total + term
        out[:, here] = total.astype(bf16)


def project_own(done, weights):
    rows = done.shape[0]
    cols, width = weights[0].shape[0] // 4, weights[0].shape[1]
    return pl.pallas_call(
        own_kernel,
        out_shape=spec(rows, cols),
        in_specs=whole(1) + [pl.BlockSpec(memory_space=pl.ANY)] * 3,
        out_specs=pl.BlockSpec(memory_space=pltpu.VMEM),
        scratch_shapes=[pltpu.VMEM((3, cols, width), bf16), pltpu.SemaphoreType.DMA((3 * OWN_STEPS,))],
        compiler_params=params(),
        cost_estimate=LIGHT,
        name="project_own",
    )(done, *weights)


def arrange_kernel(*refs):
    *blocks, out = refs
    z, x, c = spot()
    outer = jnp.where(c == 0, z, x)
    share = blocks[0].shape[1]
    for far, block in enumerate(blocks):
        at = pl.multiple_of(lax.rem(outer + 4 - far, 4) * share, share)
        for src in range(3):
            out[src, pl.ds(at, share)] = block[src]


def arrange(blocks):
    srcs, share, depth = blocks[0].shape
    return pl.pallas_call(
        arrange_kernel,
        out_shape=spec(srcs, 4 * share, depth),
        in_specs=whole(4),
        out_specs=pl.BlockSpec(memory_space=pltpu.VMEM),
        compiler_params=params(),
        cost_estimate=LIGHT,
        name="arrange",
    )(*blocks)


def column_tiles(tables, cores):
    z, x, c = spot()
    for table, mirrored in zip(tables, cores):
        core = 1 - c if mirrored else c
        half = table.shape[1]
        for start in range(0, half, BLK):
            yield table, slice(start, start + BLK), pl.ds(pl.multiple_of(core * half + start, BLK), BLK)


def others_kernel(spans, cores, *refs):
    parts, refs = refs[: len(spans)], refs[len(spans) :]
    tables, (partial, out) = refs[: len(cores)], refs[len(cores) :]
    for table, inside, at in column_tiles(tables, cores):
        total = partial[:, at].astype(f32)
        for (src, _), part in zip(spans, parts):
            total = total + nt(part[...], table[src - 1, inside])
        out[:, at] = total.astype(bf16)


def project_others(parts, tables, mirrored, partial):
    spans = tuple(part[:2] for part in parts)
    operands = [*[part[2] for part in parts], *tables, partial]
    return pl.pallas_call(
        functools.partial(others_kernel, spans, mirrored),
        out_shape=spec(*partial.shape),
        in_specs=whole(len(operands)),
        out_specs=pl.BlockSpec(memory_space=pltpu.VMEM),
        input_output_aliases={len(operands) - 1: 0},
        compiler_params=params(),
        cost_estimate=LIGHT,
        name="project_others",
    )(*operands)


def last_kernel(spans, cores, *refs):
    parts, refs = refs[: len(spans)], refs[len(spans) :]
    tables, refs = refs[: len(cores)], refs[len(cores) :]
    partial, refs = refs[0], refs[1:]
    out, tiles, sems = refs[-3:]
    made = []
    for i, ((src, start), part) in enumerate(zip(spans, parts)):
        rows = part.shape[0]
        for table, inside, at in column_tiles(tables, cores):
            total = partial[start : start + rows, at].astype(f32) + nt(part[...], table[src - 1, inside])
            slot = len(made)
            tiles[slot] = total.astype(bf16)
            made.append(pltpu.make_async_copy(tiles.at[slot], out.at[pl.ds(start, rows), at], sems.at[slot]))
            made[-1].start()
    for copy in made:
        copy.wait()


def project_last(parts, tables, mirrored, partial, held=None):
    rows = parts[0][2].shape[0]
    count = len(parts) * len(tables) * tables[0].shape[1] // BLK
    spans = tuple(part[:2] for part in parts)
    operands = [*[part[2] for part in parts], *tables, partial] + ([] if held is None else [held])
    anywhere = pl.BlockSpec(memory_space=pl.ANY)
    return pl.pallas_call(
        functools.partial(last_kernel, spans, mirrored),
        out_shape=spec(*partial.shape),
        in_specs=whole(len(parts) + len(tables) + 1) + ([] if held is None else [anywhere]),
        out_specs=anywhere,
        scratch_shapes=[pltpu.VMEM((count, rows, BLK), bf16), pltpu.SemaphoreType.DMA((count,))],
        input_output_aliases={} if held is None else {len(operands) - 1: 0},
        compiler_params=params(),
        cost_estimate=LIGHT,
        name="project_last",
    )(*operands)


def turn(a, by):
    return lax.ppermute(a, "head", [(i, (i + by) % 4) for i in range(4)])


def move(a, where):
    pairs = [(place(z, x, c), place(*where(z, x, c))) for z in range(4) for x in range(4) for c in range(2)]
    return lax.ppermute(a, "seq", pairs)


def across(a):
    return move(a, lambda z, x, c: (z, x, 1 - c))


CHIPS = [[place(z, x, c) for z in range(4) for x in range(4)] for c in range(2)]
def major(a, by):
    return move(a, lambda z, x, c: (z + by, x, c) if c == 0 else (z, x + by, c))


def tie(*groups):
    return lax.optimization_barrier(groups)


def shards(queries, key_rows, value_rows, grad_out, accepted, decay_code, w_query, w_key, w_value):
    heads = decay_code.shape[0]
    count = queries.shape[0]
    rows = float(count)
    weights = (w_query, w_key, w_value)
    raw, codes, local, message, *sent = begin(
        queries, key_rows, value_rows, grad_out, accepted, decay_code, weights, EARLY
    )
    other = across(message)
    leaving = join(rows, codes, message, other)
    share = [turn(sent[0], 1), turn(sent[1], -1), turn(sent[2], 2)]
    arrived = lax.all_to_all(leaving, "seq", 0, 0, axis_index_groups=CHIPS)
    chip_state = gather(rows, decay_code, arrived)
    theirs = across(chip_state)
    done = attend(EARLY, rows, codes, chip_state, theirs, other, local, raw)
    done, *share = tie(done, *share)
    left, right = turn(done, 1), turn(done, -1)
    total = project_own(done, weights)
    left, right, total = tie(left, right, total)
    share = jnp.stack(share)
    half = [share] + [major(share, by) for by in (1, 2, 3)]
    half, _, _ = tie(half, left, right)
    half = arrange(half)
    other_half = across(half)
    far = []
    for start in range(0, count // 2, CHUNK):
        far.append((3, start, turn(left[start : start + CHUNK], 1)))
        start += count // 2
        far.append((3, start, turn(right[start : start + CHUNK], -1)))
    sides = (1, 0, left), (2, 0, right)
    total = project_others(sides, (half,), (False,), total)
    total = project_others(sides, (other_half,), (True,), total)
    out = None
    for i in range(0, len(far), 2):
        out = project_last(far[i : i + 2], (half, other_half), (False, True), total, out)
    return out


def solution(mesh):
    in_specs = (P("seq", "head"),) * 4 + (P("seq"), P("head")) + (P(None, "head"),) * 3
    return jax.shard_map(shards, mesh=mesh, in_specs=in_specs, out_specs=P("seq", "head"), check_vma=False)
```

```python
import functools

import jax
import jax.numpy as jnp
from jax import lax
from jax.experimental import pallas as pl
from jax.experimental.pallas import tpu as pltpu
from jax.sharding import PartitionSpec as P

BLK = 256
EARLY = 512
CHUNK = 256
HDIM = 128
bf16 = jnp.bfloat16
f32 = jnp.float32
VMEM_LIMIT = 24 * 1024 * 1024
VMEM_ALL = 62 * 1024 * 1024
LIGHT = pl.CostEstimate(flops=1, bytes_accessed=1, transcendentals=0)

SHARES = 8


def place(z, x, c):
    return (z % 4) * 8 + (x % 4) * 2 + c % 2


def nt(a, b):
    return lax.dot_general(a, b, (((1,), (1,)), ((), ())), preferred_element_type=f32)


def nn(a, b):
    return lax.dot_general(a, b, (((1,), (0,)), ((), ())), preferred_element_type=f32)


def tn(a, b):
    return lax.dot_general(a, b, (((0,), (0,)), ((), ())), preferred_element_type=f32)


def spec(*shape):
    return jax.ShapeDtypeStruct(shape, bf16)


def params():
    return pltpu.CompilerParams(vmem_limit_bytes=VMEM_LIMIT)


def whole(count):
    return [pl.BlockSpec(memory_space=pltpu.VMEM)] * count


def fetch(pairs, sems):
    copies = [pltpu.make_async_copy(source, target, sems.at[i]) for i, (source, target) in enumerate(pairs)]
    for copy in copies:
        copy.start()
    return copies


def begin_kernel(
    cut, q, k, v, g, accepted, decay_code, wq, wk, wv, raw, codes, local, message, s1, s2, s3, raw_g, keep, sems
):
    width = q.shape[1]
    rows = raw.shape[0]
    pairs = [(g, raw_g), (accepted, keep)]
    for part, ref in enumerate((q, k, v)):
        pairs.append((ref, raw.at[:, pl.ds(part * width, width)]))
    y = lax.axis_index("head")
    z, x, c = spot()
    piece = c * 4 + jnp.where(c == 0, z, x)
    for out, by in zip((s1, s2, s3), (1, 3, 2)):
        for part, w in enumerate((wq, wk, wv)):
            pairs.append((w.at[lax.rem(y + by, 4), piece], out.at[:, pl.ds(part * width, width)]))
    copies = fetch(pairs, sems)
    line = lax.broadcasted_iota(jnp.int32, codes.shape, 0)
    filled = jnp.zeros(codes.shape, f32)
    for head in range(decay_code.shape[0]):
        filled = jnp.where(line == head, decay_code[head].astype(f32), filled)
    codes[...] = filled.astype(bf16)
    for copy in copies[:2]:
        copy.wait()
    column = jnp.broadcast_to(keep[0:1, :].astype(f32), (HDIM, rows)).T
    wide = jnp.concatenate([column] * (width // HDIM), axis=1)
    raw[:, 3 * width :] = (raw_g[...].astype(f32) * wide).astype(bf16)
    for copy in copies[2:]:
        copy.wait()
    for head in range(local.shape[2]):
        rate = jnp.exp2(-0.5 * jnp.full((1, HDIM), decay_code[head], f32))
        found, spans = [], []
        for half, (low, high) in enumerate(((0, cut), (cut, rows))):
            where = lax.broadcasted_iota(jnp.int32, (high - low, HDIM), 0).astype(f32)
            to_end = jnp.exp(-rate * (high - low - 1.0 - where))
            from_start = jnp.exp(-rate * where)
            spans.append(jnp.exp(-rate * (high - low)))
            at = lambda part: raw[low:high, part * width + head * HDIM : part * width + (head + 1) * HDIM]
            kv = tn((at(1).astype(f32) * to_end).astype(bf16), at(2))
            qg = tn((at(0).astype(f32) * from_start).astype(bf16), at(3))
            found.append((kv, qg))
            local[half, 0, head] = kv
            local[half, 1, head] = qg
        message[0, head] = (spans[1] * found[0][0] + found[1][0]).astype(bf16)
        message[1, head] = (found[0][1] + spans[0] * found[1][1]).astype(bf16)


def begin(q, k, v, g, accepted, decay_code, weights, early):
    rows, width = q.shape
    out_rows = weights[0].shape[0]
    share = out_rows // (4 * SHARES)
    shaped = [w.reshape(4, SHARES, share, width) for w in weights]
    heads = decay_code.shape[0]
    far = pl.BlockSpec(memory_space=pl.ANY)
    return pl.pallas_call(
        functools.partial(begin_kernel, early),
        out_shape=[
            spec(rows, 4 * width),
            spec(16, HDIM),
            jax.ShapeDtypeStruct((2, 2, heads, HDIM, HDIM), f32),
            spec(2, heads, HDIM, HDIM),
            *[spec(share, 3 * width)] * 3,
        ],
        in_specs=[far] * 5 + [pl.BlockSpec(memory_space=pltpu.SMEM)] + [far] * 3,
        out_specs=whole(7),
        scratch_shapes=[
            pltpu.VMEM((rows, width), bf16),
            pltpu.VMEM((1, rows), jnp.int32),
            pltpu.SemaphoreType.DMA((14,)),
        ],
        compiler_params=pltpu.CompilerParams(vmem_limit_bytes=VMEM_ALL),
        cost_estimate=LIGHT,
        name="begin",
    )(q, k, v, g, accepted.reshape(1, rows), decay_code, *shaped)


def spot():
    seq = lax.axis_index("seq")
    return lax.div(seq, 8), lax.rem(lax.div(seq, 2), 4), lax.rem(seq, 2)


def fade(codes, head, span, count):
    rate = jnp.exp2(-0.5 * codes[head : head + 1, :].astype(f32))
    faded = jnp.exp(-rate * (span * jnp.maximum(count, 0).astype(f32)))
    return jnp.where(count >= 0, faded, 0.0)


def join_kernel(rows, codes_at, mine_at, other_at, out, codes, mine, other, sems):
    z, x, c = spot()
    late = c == 1
    chip = z * 4 + x
    for copy in fetch([(codes_at, codes), (mine_at, mine), (other_at, other)], sems):
        copy.wait()
    for head in range(mine.shape[1]):
        one = fade(codes, head, rows, jnp.int32(1))
        near, far = mine[:, head].astype(f32), other[:, head].astype(f32)
        before, after = jnp.where(late, far, near), jnp.where(late, near, far)
        kv = (one * before[0] + after[0]).astype(bf16)
        qg = (before[1] + one * after[1]).astype(bf16)
        for to in range(out.shape[0]):

            @pl.when(c == head)
            def _(to=to, kv=kv, qg=qg):
                out[to, 0] = jnp.where(to > chip, kv, qg)


def join(rows, codes, mine, other):
    return pl.pallas_call(
        functools.partial(join_kernel, rows),
        out_shape=spec(16, 1, *mine.shape[2:]),
        in_specs=[pl.BlockSpec(memory_space=pl.ANY)] * 3,
        out_specs=pl.BlockSpec(memory_space=pltpu.VMEM),
        scratch_shapes=[
            pltpu.VMEM(codes.shape, bf16),
            pltpu.VMEM(mine.shape, bf16),
            pltpu.VMEM(other.shape, bf16),
            pltpu.SemaphoreType.DMA((3,)),
        ],
        compiler_params=pltpu.CompilerParams(vmem_limit_bytes=VMEM_ALL),
        cost_estimate=LIGHT,
        name="join",
    )(codes, mine, other)


def gather_kernel(rows, decay_code, arrived, out):
    z, x, c = spot()
    chip = z * 4 + x
    kv = qg = jnp.zeros((HDIM, HDIM), f32)
    code = jnp.full((1, HDIM), jnp.where(c == 0, decay_code[0], decay_code[1]), jnp.int32)
    for there in range(arrived.shape[0]):
        it = arrived[there, 0].astype(f32)
        kv += it * fade(code, 0, 2 * rows, chip - 1 - there)
        qg += it * fade(code, 0, 2 * rows, there - chip - 1)
    out[0] = kv.astype(bf16)
    out[1] = qg.astype(bf16)


def enter_states(early, rows, codes, mine, theirs, other, local, state0, state1):
    z, x, c = spot()
    late = c == 1
    heads = other.shape[1]
    width = heads * HDIM
    for head in range(heads):
        kv = jnp.where(c == head, mine[0], theirs[0]).astype(f32)
        qg = jnp.where(c == head, mine[1], theirs[1]).astype(f32)
        one = fade(codes, head, rows, jnp.int32(1))
        start = fade(codes, head, early, jnp.int32(1))
        end = fade(codes, head, rows - early, jnp.int32(1))
        kv = jnp.where(late, one * kv + other[0, head].astype(f32), kv)
        qg = jnp.where(late, qg, one * qg + other[1, head].astype(f32))
        here = pl.ds(head * HDIM, HDIM)
        there = pl.ds(width + head * HDIM, HDIM)
        state0[here] = kv.astype(bf16)
        state0[there] = (end * qg + local[1, 1, head]).astype(bf16)
        state1[here] = (start * kv + local[0, 0, head]).astype(bf16)
        state1[there] = qg.astype(bf16)
    state0[2 * width :] = codes[...]
    state1[2 * width :] = codes[...]


def gather(rows, decay_code, arrived):
    return pl.pallas_call(
        functools.partial(gather_kernel, rows),
        out_shape=spec(2, HDIM, HDIM),
        in_specs=[pl.BlockSpec(memory_space=pltpu.SMEM), pl.BlockSpec(memory_space=pltpu.VMEM)],
        out_specs=pl.BlockSpec(memory_space=pltpu.VMEM),
        compiler_params=params(),
        cost_estimate=LIGHT,
        name="gather",
    )(decay_code, arrived)


def attend_rows(raws, codes, out_rows, first_row, targets):
    width = raws[0].shape[1] // 4
    heads = width // HDIM
    rows = out_rows
    starts = list(range(0, rows, BLK))
    sizes = [min(BLK, rows - start) for start in starts]
    count = len(starts)
    edges = [0]
    for raw in raws:
        edges.append(edges[-1] + raw.shape[0])

    def take(block, part, head):
        low, high = starts[block], starts[block] + sizes[block]
        here = slice(part * width + head * HDIM, part * width + (head + 1) * HDIM)
        found = []
        for raw, start, end in zip(raws, edges, edges[1:]):
            if max(low, start) < min(high, end):
                found.append(raw[max(low, start) - start : min(high, end) - start, here])
        return found[0] if len(found) == 1 else jnp.concatenate(found, axis=0)

    def table(rate1, later, earlier, flip):
        shape = (sizes[earlier], sizes[later]) if flip else (sizes[later], sizes[earlier])
        row = lax.broadcasted_iota(jnp.int32, shape, 0)
        col = lax.broadcasted_iota(jnp.int32, shape, 1)
        rate = rate1 if shape[1] == HDIM else jnp.concatenate([rate1] * (shape[1] // HDIM), axis=1)
        gap = (col - row if flip else row - col).astype(f32)
        if later == earlier:
            return jnp.where(gap >= 0, jnp.exp(-rate * jnp.maximum(gap, 0.0)), 0.0)
        return jnp.exp(-rate * (starts[later] - starts[earlier] + gap))

    cut = lambda a, d: (a * d).astype(bf16)
    for head in range(heads):
        rate = jnp.exp2(-0.5 * codes[head : head + 1, :].astype(f32))
        made = {}

        def decay(later, earlier, flip):
            key = (starts[later] - starts[earlier], sizes[later], sizes[earlier], flip)
            if key not in made:
                made[key] = table(rate, later, earlier, flip)
            return made[key]

        q, k, v, g = ([take(block, part, head) for block in range(count)] for part in range(4))
        for block in range(count):
            start, size = starts[block], sizes[block]
            dq = dk = dv = jnp.zeros((size, HDIM), f32)
            for other in range(block + 1):
                dq += nn(cut(nt(g[block], v[other]), decay(block, other, False)), k[other])
            for other in range(block, count):
                dk += nn(cut(nt(v[block], g[other]), decay(other, block, True)), q[other])
                dv += nn(cut(nt(k[block], q[other]), decay(other, block, True)), g[other])
            for part, value in enumerate((dq, dk, dv)):
                here = pl.ds(part * width + head * HDIM, HDIM)
                value = value.astype(bf16)
                low = first_row + start
                for ref, begins in targets:
                    from_row, to_row = max(low, begins), min(low + size, begins + ref.shape[0])
                    if from_row < to_row:
                        ref[from_row - begins : to_row - begins, here] = value[from_row - low : to_row - low]


def inside_kernel(early, codes_at, raw_at, out, codes, raw, made, sems, out_sems):
    copies = fetch([(codes_at, codes), (raw_at, raw)], sems)
    for copy in copies:
        copy.wait()
    count = made.shape[0]
    written = []
    for i, (low, high) in enumerate(((0, early), (early, count))):
        attend_rows([raw.at[low:high]], codes, high - low, low, [(made, 0)])
        written.append(pltpu.make_async_copy(made.at[low:high], out.at[low:high], out_sems.at[i]))
        written[-1].start()
    for copy in written:
        copy.wait()


def inside(early, codes, raw):
    count, depth = raw.shape[0], raw.shape[1] // 4 * 3
    anywhere = pl.BlockSpec(memory_space=pl.ANY)
    return pl.pallas_call(
        functools.partial(inside_kernel, early),
        out_shape=spec(count, depth),
        in_specs=[anywhere] * 2,
        out_specs=anywhere,
        scratch_shapes=[
            pltpu.VMEM(codes.shape, bf16),
            pltpu.VMEM(raw.shape, bf16),
            pltpu.VMEM((count, depth), bf16),
            pltpu.SemaphoreType.DMA((2,)),
            pltpu.SemaphoreType.DMA((2,)),
        ],
        compiler_params=pltpu.CompilerParams(vmem_limit_bytes=VMEM_ALL),
        cost_estimate=LIGHT,
        name="inside",
    )(codes, raw)


def attend_kernel(early, rows, *refs):
    inputs, out, rest = refs[:7], refs[7], refs[8:]
    held, (state0, state1, sems, out_sems) = rest[:7], rest[7:]
    copies = fetch(list(zip(inputs, held)), sems)
    for copy in copies[:5]:
        copy.wait()
    codes, raw, made = held[0], held[5], held[6]
    count, width = made.shape[0], made.shape[1] // 3
    enter_states(float(early), rows, *held[:5], state0, state1)
    for copy in copies[5:]:
        copy.wait()
    written = []
    for i, (low, high, state) in enumerate(((0, early, state0), (early, count, state1))):
        where = lax.broadcasted_iota(jnp.int32, (high - low, HDIM), 0).astype(f32)
        for head in range(width // HDIM):
            rate = jnp.exp2(-0.5 * codes[head : head + 1, :].astype(f32))
            lead, lag = jnp.exp(-rate * (where + 1.0)), jnp.exp(-rate * (high - low - where))
            k, v, g = (raw[low:high, part * width + head * HDIM : part * width + (head + 1) * HDIM] for part in (1, 2, 3))
            kv = state[head * HDIM : (head + 1) * HDIM, :]
            qg = state[width + head * HDIM : width + (head + 1) * HDIM, :]
            for part, value in enumerate((lead * nt(g, kv), lag * nt(v, qg), lag * nn(k, qg))):
                here = pl.ds(part * width + head * HDIM, HDIM)
                made[low:high, here] = (made[low:high, here].astype(f32) + value).astype(bf16)
        written.append(pltpu.make_async_copy(made.at[low:high], out.at[low:high], out_sems.at[i]))
        written[-1].start()
    for copy in written:
        copy.wait()


def attend(early, rows, codes, mine, theirs, other, local, raw, made):
    operands = (codes, mine, theirs, other, local, raw, made)
    state = pltpu.VMEM((2 * other.shape[1] * HDIM + codes.shape[0], HDIM), bf16)
    anywhere = pl.BlockSpec(memory_space=pl.ANY)
    return pl.pallas_call(
        functools.partial(attend_kernel, early, rows),
        out_shape=spec(*made.shape),
        in_specs=[anywhere] * 7,
        out_specs=anywhere,
        scratch_shapes=[pltpu.VMEM(a.shape, a.dtype) for a in operands]
        + [state, state, pltpu.SemaphoreType.DMA((7,)), pltpu.SemaphoreType.DMA((2,))],
        compiler_params=pltpu.CompilerParams(vmem_limit_bytes=VMEM_ALL),
        cost_estimate=LIGHT,
        name="attend",
    )(*operands)


OWN_STEPS = 4


def own_kernel(done, wq, wk, wv, out, w, sems):
    y = lax.axis_index("head")
    cols, width = w.shape[1:]
    part = cols // OWN_STEPS
    pairs = []
    for step in range(OWN_STEPS):
        begins = pl.multiple_of(y * cols + step * part, part)
        pairs += [(ref.at[pl.ds(begins, part)], w.at[i, pl.ds(step * part, part)]) for i, ref in enumerate((wq, wk, wv))]
    copies = fetch(pairs, sems)
    for step in range(OWN_STEPS):
        for copy in copies[3 * step : 3 * step + 3]:
            copy.wait()
        here = slice(step * part, (step + 1) * part)
        total = None
        for i in range(3):
            term = nt(done[:, i * width : (i + 1) * width], w[i, here])
            total = term if total is None else total + term
        out[:, here] = total.astype(bf16)


def project_own(done, weights):
    rows = done.shape[0]
    cols, width = weights[0].shape[0] // 4, weights[0].shape[1]
    return pl.pallas_call(
        own_kernel,
        out_shape=spec(rows, cols),
        in_specs=whole(1) + [pl.BlockSpec(memory_space=pl.ANY)] * 3,
        out_specs=pl.BlockSpec(memory_space=pltpu.VMEM),
        scratch_shapes=[pltpu.VMEM((3, cols, width), bf16), pltpu.SemaphoreType.DMA((3 * OWN_STEPS,))],
        compiler_params=params(),
        cost_estimate=LIGHT,
        name="project_own",
    )(done, *weights)


def arrange_kernel(*refs):
    *blocks, out = refs
    z, x, c = spot()
    outer = jnp.where(c == 0, z, x)
    share = blocks[0].shape[1]
    for far, block in enumerate(blocks):
        at = pl.multiple_of(lax.rem(outer + 4 - far, 4) * share, share)
        for src in range(3):
            out[src, pl.ds(at, share)] = block[src]


def arrange(blocks):
    srcs, share, depth = blocks[0].shape
    return pl.pallas_call(
        arrange_kernel,
        out_shape=spec(srcs, 4 * share, depth),
        in_specs=whole(4),
        out_specs=pl.BlockSpec(memory_space=pltpu.VMEM),
        compiler_params=params(),
        cost_estimate=LIGHT,
        name="arrange",
    )(*blocks)


def column_tiles(tables, cores):
    z, x, c = spot()
    for table, mirrored in zip(tables, cores):
        core = 1 - c if mirrored else c
        half = table.shape[1]
        for start in range(0, half, BLK):
            yield table, slice(start, start + BLK), pl.ds(pl.multiple_of(core * half + start, BLK), BLK)


def others_kernel(spans, cores, *refs):
    parts, refs = refs[: len(spans)], refs[len(spans) :]
    tables, (partial, out) = refs[: len(cores)], refs[len(cores) :]
    for table, inside, at in column_tiles(tables, cores):
        total = partial[:, at].astype(f32)
        for (src, _), part in zip(spans, parts):
            total = total + nt(part[...], table[src - 1, inside])
        out[:, at] = total.astype(bf16)


def project_others(parts, tables, mirrored, partial):
    spans = tuple(part[:2] for part in parts)
    operands = [*[part[2] for part in parts], *tables, partial]
    return pl.pallas_call(
        functools.partial(others_kernel, spans, mirrored),
        out_shape=spec(*partial.shape),
        in_specs=whole(len(operands)),
        out_specs=pl.BlockSpec(memory_space=pltpu.VMEM),
        input_output_aliases={len(operands) - 1: 0},
        compiler_params=params(),
        cost_estimate=LIGHT,
        name="project_others",
    )(*operands)


def last_kernel(spans, cores, *refs):
    parts, refs = refs[: len(spans)], refs[len(spans) :]
    tables, refs = refs[: len(cores)], refs[len(cores) :]
    partial, refs = refs[0], refs[1:]
    out, tiles, sems = refs[-3:]
    made = []
    for i, ((src, start), part) in enumerate(zip(spans, parts)):
        rows = part.shape[0]
        for table, inside, at in column_tiles(tables, cores):
            total = partial[start : start + rows, at].astype(f32) + nt(part[...], table[src - 1, inside])
            slot = len(made)
            tiles[slot] = total.astype(bf16)
            made.append(pltpu.make_async_copy(tiles.at[slot], out.at[pl.ds(start, rows), at], sems.at[slot]))
            made[-1].start()
    for copy in made:
        copy.wait()


def project_last(parts, tables, mirrored, partial, held=None):
    rows = parts[0][2].shape[0]
    count = len(parts) * len(tables) * tables[0].shape[1] // BLK
    spans = tuple(part[:2] for part in parts)
    operands = [*[part[2] for part in parts], *tables, partial] + ([] if held is None else [held])
    anywhere = pl.BlockSpec(memory_space=pl.ANY)
    return pl.pallas_call(
        functools.partial(last_kernel, spans, mirrored),
        out_shape=spec(*partial.shape),
        in_specs=whole(len(parts) + len(tables) + 1) + ([] if held is None else [anywhere]),
        out_specs=anywhere,
        scratch_shapes=[pltpu.VMEM((count, rows, BLK), bf16), pltpu.SemaphoreType.DMA((count,))],
        input_output_aliases={} if held is None else {len(operands) - 1: 0},
        compiler_params=params(),
        cost_estimate=LIGHT,
        name="project_last",
    )(*operands)


def turn(a, by):
    return lax.ppermute(a, "head", [(i, (i + by) % 4) for i in range(4)])


def move(a, where):
    pairs = [(place(z, x, c), place(*where(z, x, c))) for z in range(4) for x in range(4) for c in range(2)]
    return lax.ppermute(a, "seq", pairs)


def across(a):
    return move(a, lambda z, x, c: (z, x, 1 - c))


CHIPS = [[place(z, x, c) for z in range(4) for x in range(4)] for c in range(2)]
def major(a, by):
    return move(a, lambda z, x, c: (z + by, x, c) if c == 0 else (z, x + by, c))


def tie(*groups):
    return lax.optimization_barrier(groups)


def shards(queries, key_rows, value_rows, grad_out, accepted, decay_code, w_query, w_key, w_value):
    heads = decay_code.shape[0]
    count = queries.shape[0]
    rows = float(count)
    weights = (w_query, w_key, w_value)
    raw, codes, local, message, *sent = begin(
        queries, key_rows, value_rows, grad_out, accepted, decay_code, weights, EARLY
    )
    other = across(message)
    leaving = join(rows, codes, message, other)
    share = [turn(sent[0], 1), turn(sent[1], -1), turn(sent[2], 2)]
    arrived = lax.all_to_all(leaving, "seq", 0, 0, axis_index_groups=CHIPS)
    held, leaving = tie((codes, raw), leaving)
    arrived, made = tie(arrived, inside(EARLY, *held))
    chip_state = gather(rows, decay_code, arrived)
    theirs = across(chip_state)
    done = attend(EARLY, rows, codes, chip_state, theirs, other, local, raw, made)
    done, *share = tie(done, *share)
    left, right = turn(done, 1), turn(done, -1)
    total = project_own(done, weights)
    left, right, total = tie(left, right, total)
    share = jnp.stack(share)
    half = [share] + [major(share, by) for by in (1, 2, 3)]
    half, _, _ = tie(half, left, right)
    half = arrange(half)
    other_half = across(half)
    far = []
    for start in range(0, count // 2, CHUNK):
        far.append((3, start, turn(left[start : start + CHUNK], 1)))
        start += count // 2
        far.append((3, start, turn(right[start : start + CHUNK], -1)))
    sides = (1, 0, left), (2, 0, right)
    total = project_others(sides, (half,), (False,), total)
    total = project_others(sides, (other_half,), (True,), total)
    out = None
    for i in range(0, len(far), 2):
        out = project_last(far[i : i + 2], (half, other_half), (False, True), total, out)
    return out


def solution(mesh):
    in_specs = (P("seq", "head"),) * 4 + (P("seq"), P("head")) + (P(None, "head"),) * 3
    return jax.shard_map(shards, mesh=mesh, in_specs=in_specs, out_specs=P("seq", "head"), check_vma=False)
```

```python
import functools

import jax
import jax.numpy as jnp
from jax import lax
from jax.experimental import pallas as pl
from jax.experimental.pallas import tpu as pltpu
from jax.sharding import PartitionSpec as P

BLK = 256
EARLY = 512
CHUNK = 256
HDIM = 128
bf16 = jnp.bfloat16
f32 = jnp.float32
VMEM_LIMIT = 24 * 1024 * 1024
VMEM_ALL = 62 * 1024 * 1024
LIGHT = pl.CostEstimate(flops=1, bytes_accessed=1, transcendentals=0)

SHARES = 8


def place(z, x, c):
    return (z % 4) * 8 + (x % 4) * 2 + c % 2


def nt(a, b):
    return lax.dot_general(a, b, (((1,), (1,)), ((), ())), preferred_element_type=f32)


def nn(a, b):
    return lax.dot_general(a, b, (((1,), (0,)), ((), ())), preferred_element_type=f32)


def tn(a, b):
    return lax.dot_general(a, b, (((0,), (0,)), ((), ())), preferred_element_type=f32)


def spec(*shape):
    return jax.ShapeDtypeStruct(shape, bf16)


def params():
    return pltpu.CompilerParams(vmem_limit_bytes=VMEM_LIMIT)


def whole(count):
    return [pl.BlockSpec(memory_space=pltpu.VMEM)] * count


def fetch(pairs, sems):
    copies = [pltpu.make_async_copy(source, target, sems.at[i]) for i, (source, target) in enumerate(pairs)]
    for copy in copies:
        copy.start()
    return copies


def begin_kernel(
    cut, q, k, v, g, accepted, decay_code, wq, wk, wv, raw, codes, local, message, s1, s2, s3, raw_g, keep, sems
):
    width = q.shape[1]
    rows = raw.shape[0]
    pairs = [(g, raw_g), (accepted, keep)]
    for part, ref in enumerate((q, k, v)):
        pairs.append((ref, raw.at[:, pl.ds(part * width, width)]))
    y = lax.axis_index("head")
    z, x, c = spot()
    piece = c * 4 + jnp.where(c == 0, z, x)
    for out, by in zip((s1, s2, s3), (1, 3, 2)):
        for part, w in enumerate((wq, wk, wv)):
            pairs.append((w.at[lax.rem(y + by, 4), piece], out.at[:, pl.ds(part * width, width)]))
    copies = fetch(pairs, sems)
    line = lax.broadcasted_iota(jnp.int32, codes.shape, 0)
    filled = jnp.zeros(codes.shape, f32)
    for head in range(decay_code.shape[0]):
        filled = jnp.where(line == head, decay_code[head].astype(f32), filled)
    codes[...] = filled.astype(bf16)
    for copy in copies[:2]:
        copy.wait()
    column = jnp.broadcast_to(keep[0:1, :].astype(f32), (HDIM, rows)).T
    wide = jnp.concatenate([column] * (width // HDIM), axis=1)
    raw[:, 3 * width :] = (raw_g[...].astype(f32) * wide).astype(bf16)
    for copy in copies[2:]:
        copy.wait()
    for head in range(local.shape[2]):
        rate = jnp.exp2(-0.5 * jnp.full((1, HDIM), decay_code[head], f32))
        found, spans = [], []
        for half, (low, high) in enumerate(((0, cut), (cut, rows))):
            where = lax.broadcasted_iota(jnp.int32, (high - low, HDIM), 0).astype(f32)
            to_end = jnp.exp(-rate * (high - low - 1.0 - where))
            from_start = jnp.exp(-rate * where)
            spans.append(jnp.exp(-rate * (high - low)))
            at = lambda part: raw[low:high, part * width + head * HDIM : part * width + (head + 1) * HDIM]
            kv = tn((at(1).astype(f32) * to_end).astype(bf16), at(2))
            qg = tn((at(0).astype(f32) * from_start).astype(bf16), at(3))
            found.append((kv, qg))
            local[half, 0, head] = kv
            local[half, 1, head] = qg
        message[0, head] = (spans[1] * found[0][0] + found[1][0]).astype(bf16)
        message[1, head] = (found[0][1] + spans[0] * found[1][1]).astype(bf16)


def begin(q, k, v, g, accepted, decay_code, weights, early):
    rows, width = q.shape
    out_rows = weights[0].shape[0]
    share = out_rows // (4 * SHARES)
    shaped = [w.reshape(4, SHARES, share, width) for w in weights]
    heads = decay_code.shape[0]
    far = pl.BlockSpec(memory_space=pl.ANY)
    return pl.pallas_call(
        functools.partial(begin_kernel, early),
        out_shape=[
            spec(rows, 4 * width),
            spec(16, HDIM),
            jax.ShapeDtypeStruct((2, 2, heads, HDIM, HDIM), f32),
            spec(2, heads, HDIM, HDIM),
            *[spec(share, 3 * width)] * 3,
        ],
        in_specs=[far] * 5 + [pl.BlockSpec(memory_space=pltpu.SMEM)] + [far] * 3,
        out_specs=whole(7),
        scratch_shapes=[
            pltpu.VMEM((rows, width), bf16),
            pltpu.VMEM((1, rows), jnp.int32),
            pltpu.SemaphoreType.DMA((14,)),
        ],
        compiler_params=pltpu.CompilerParams(vmem_limit_bytes=VMEM_ALL),
        cost_estimate=LIGHT,
        name="begin",
    )(q, k, v, g, accepted.reshape(1, rows), decay_code, *shaped)


def spot():
    seq = lax.axis_index("seq")
    return lax.div(seq, 8), lax.rem(lax.div(seq, 2), 4), lax.rem(seq, 2)


def fade(codes, head, span, count):
    rate = jnp.exp2(-0.5 * codes[head : head + 1, :].astype(f32))
    faded = jnp.exp(-rate * (span * jnp.maximum(count, 0).astype(f32)))
    return jnp.where(count >= 0, faded, 0.0)


def join_kernel(rows, codes_at, mine_at, other_at, out, codes, mine, other, sems):
    z, x, c = spot()
    late = c == 1
    chip = z * 4 + x
    for copy in fetch([(codes_at, codes), (mine_at, mine), (other_at, other)], sems):
        copy.wait()
    for head in range(mine.shape[1]):
        one = fade(codes, head, rows, jnp.int32(1))
        near, far = mine[:, head].astype(f32), other[:, head].astype(f32)
        before, after = jnp.where(late, far, near), jnp.where(late, near, far)
        kv = (one * before[0] + after[0]).astype(bf16)
        qg = (before[1] + one * after[1]).astype(bf16)
        for to in range(out.shape[0]):

            @pl.when(c == head)
            def _(to=to, kv=kv, qg=qg):
                out[to, 0] = jnp.where(to > chip, kv, qg)


def join(rows, codes, mine, other):
    return pl.pallas_call(
        functools.partial(join_kernel, rows),
        out_shape=spec(16, 1, *mine.shape[2:]),
        in_specs=[pl.BlockSpec(memory_space=pl.ANY)] * 3,
        out_specs=pl.BlockSpec(memory_space=pltpu.VMEM),
        scratch_shapes=[
            pltpu.VMEM(codes.shape, bf16),
            pltpu.VMEM(mine.shape, bf16),
            pltpu.VMEM(other.shape, bf16),
            pltpu.SemaphoreType.DMA((3,)),
        ],
        compiler_params=pltpu.CompilerParams(vmem_limit_bytes=VMEM_ALL),
        cost_estimate=LIGHT,
        name="join",
    )(codes, mine, other)


def gather_kernel(rows, decay_code, arrived, out):
    z, x, c = spot()
    chip = z * 4 + x
    kv = qg = jnp.zeros((HDIM, HDIM), f32)
    code = jnp.full((1, HDIM), jnp.where(c == 0, decay_code[0], decay_code[1]), jnp.int32)
    for there in range(arrived.shape[0]):
        it = arrived[there, 0].astype(f32)
        kv += it * fade(code, 0, 2 * rows, chip - 1 - there)
        qg += it * fade(code, 0, 2 * rows, there - chip - 1)
    out[0] = kv.astype(bf16)
    out[1] = qg.astype(bf16)


def enter_states(early, rows, codes, mine, theirs, other, local, state0, state1):
    z, x, c = spot()
    late = c == 1
    heads = other.shape[1]
    width = heads * HDIM
    for head in range(heads):
        kv = jnp.where(c == head, mine[0], theirs[0]).astype(f32)
        qg = jnp.where(c == head, mine[1], theirs[1]).astype(f32)
        one = fade(codes, head, rows, jnp.int32(1))
        start = fade(codes, head, early, jnp.int32(1))
        end = fade(codes, head, rows - early, jnp.int32(1))
        kv = jnp.where(late, one * kv + other[0, head].astype(f32), kv)
        qg = jnp.where(late, qg, one * qg + other[1, head].astype(f32))
        here = pl.ds(head * HDIM, HDIM)
        there = pl.ds(width + head * HDIM, HDIM)
        state0[here] = kv.astype(bf16)
        state0[there] = (end * qg + local[1, 1, head]).astype(bf16)
        state1[here] = (start * kv + local[0, 0, head]).astype(bf16)
        state1[there] = qg.astype(bf16)
    state0[2 * width :] = codes[...]
    state1[2 * width :] = codes[...]


def gather(rows, decay_code, arrived):
    return pl.pallas_call(
        functools.partial(gather_kernel, rows),
        out_shape=spec(2, HDIM, HDIM),
        in_specs=[pl.BlockSpec(memory_space=pltpu.SMEM), pl.BlockSpec(memory_space=pltpu.VMEM)],
        out_specs=pl.BlockSpec(memory_space=pltpu.VMEM),
        compiler_params=params(),
        cost_estimate=LIGHT,
        name="gather",
    )(decay_code, arrived)


def attend_rows(raws, codes, out_rows, first_row, targets):
    width = raws[0].shape[1] // 4
    heads = width // HDIM
    rows = out_rows
    starts = list(range(0, rows, BLK))
    sizes = [min(BLK, rows - start) for start in starts]
    count = len(starts)
    edges = [0]
    for raw in raws:
        edges.append(edges[-1] + raw.shape[0])

    def take(block, part, head):
        low, high = starts[block], starts[block] + sizes[block]
        here = slice(part * width + head * HDIM, part * width + (head + 1) * HDIM)
        found = []
        for raw, start, end in zip(raws, edges, edges[1:]):
            if max(low, start) < min(high, end):
                found.append(raw[max(low, start) - start : min(high, end) - start, here])
        return found[0] if len(found) == 1 else jnp.concatenate(found, axis=0)

    def table(rate1, later, earlier, flip):
        shape = (sizes[earlier], sizes[later]) if flip else (sizes[later], sizes[earlier])
        row = lax.broadcasted_iota(jnp.int32, shape, 0)
        col = lax.broadcasted_iota(jnp.int32, shape, 1)
        rate = rate1 if shape[1] == HDIM else jnp.concatenate([rate1] * (shape[1] // HDIM), axis=1)
        gap = (col - row if flip else row - col).astype(f32)
        if later == earlier:
            return jnp.where(gap >= 0, jnp.exp(-rate * jnp.maximum(gap, 0.0)), 0.0)
        return jnp.exp(-rate * (starts[later] - starts[earlier] + gap))

    cut = lambda a, d: (a * d).astype(bf16)
    for head in range(heads):
        rate = jnp.exp2(-0.5 * codes[head : head + 1, :].astype(f32))
        made = {}

        def decay(later, earlier, flip):
            key = (starts[later] - starts[earlier], sizes[later], sizes[earlier], flip)
            if key not in made:
                made[key] = table(rate, later, earlier, flip)
            return made[key]

        q, k, v, g = ([take(block, part, head) for block in range(count)] for part in range(4))
        for block in range(count):
            start, size = starts[block], sizes[block]
            dq = dk = dv = jnp.zeros((size, HDIM), f32)
            for other in range(block + 1):
                dq += nn(cut(nt(g[block], v[other]), decay(block, other, False)), k[other])
            for other in range(block, count):
                dk += nn(cut(nt(v[block], g[other]), decay(other, block, True)), q[other])
                dv += nn(cut(nt(k[block], q[other]), decay(other, block, True)), g[other])
            for part, value in enumerate((dq, dk, dv)):
                here = pl.ds(part * width + head * HDIM, HDIM)
                value = value.astype(bf16)
                low = first_row + start
                for ref, begins in targets:
                    from_row, to_row = max(low, begins), min(low + size, begins + ref.shape[0])
                    if from_row < to_row:
                        ref[from_row - begins : to_row - begins, here] = value[from_row - low : to_row - low]


def inside_kernel(early, codes_at, raw_at, out, codes, raw, made, sems, out_sems):
    copies = fetch([(codes_at, codes), (raw_at, raw)], sems)
    for copy in copies:
        copy.wait()
    count = made.shape[0]
    written = []
    for i, (low, high) in enumerate(((0, early), (early, count))):
        attend_rows([raw.at[low:high]], codes, high - low, low, [(made, 0)])
        written.append(pltpu.make_async_copy(made.at[low:high], out.at[low:high], out_sems.at[i]))
        written[-1].start()
    for copy in written:
        copy.wait()


def inside(early, codes, raw):
    count, depth = raw.shape[0], raw.shape[1] // 4 * 3
    anywhere = pl.BlockSpec(memory_space=pl.ANY)
    return pl.pallas_call(
        functools.partial(inside_kernel, early),
        out_shape=spec(count, depth),
        in_specs=[anywhere] * 2,
        out_specs=anywhere,
        scratch_shapes=[
            pltpu.VMEM(codes.shape, bf16),
            pltpu.VMEM(raw.shape, bf16),
            pltpu.VMEM((count, depth), bf16),
            pltpu.SemaphoreType.DMA((2,)),
            pltpu.SemaphoreType.DMA((2,)),
        ],
        compiler_params=pltpu.CompilerParams(vmem_limit_bytes=VMEM_ALL),
        cost_estimate=LIGHT,
        name="inside",
    )(codes, raw)


def attend_kernel(early, rows, *refs):
    inputs, out, rest = refs[:7], refs[7], refs[8:]
    held, (state0, state1, sems, out_sems) = rest[:7], rest[7:]
    pairs = list(zip(inputs[:5], held[:5]))
    for part in (slice(0, early), slice(early, None)):
        pairs += [(source.at[part], target.at[part]) for source, target in zip(inputs[5:], held[5:])]
    copies = fetch(pairs, sems)
    for copy in copies[:5]:
        copy.wait()
    codes, raw, made = held[0], held[5], held[6]
    count, width = made.shape[0], made.shape[1] // 3
    enter_states(float(early), rows, *held[:5], state0, state1)
    written = []
    for i, (low, high, state) in enumerate(((0, early, state0), (early, count, state1))):
        for copy in copies[5 + 2 * i : 7 + 2 * i]:
            copy.wait()
        where = lax.broadcasted_iota(jnp.int32, (high - low, HDIM), 0).astype(f32)
        for head in range(width // HDIM):
            rate = jnp.exp2(-0.5 * codes[head : head + 1, :].astype(f32))
            lead, lag = jnp.exp(-rate * (where + 1.0)), jnp.exp(-rate * (high - low - where))
            k, v, g = (raw[low:high, part * width + head * HDIM : part * width + (head + 1) * HDIM] for part in (1, 2, 3))
            kv = state[head * HDIM : (head + 1) * HDIM, :]
            qg = state[width + head * HDIM : width + (head + 1) * HDIM, :]
            for part, value in enumerate((lead * nt(g, kv), lag * nt(v, qg), lag * nn(k, qg))):
                here = pl.ds(part * width + head * HDIM, HDIM)
                made[low:high, here] = (made[low:high, here].astype(f32) + value).astype(bf16)
        written.append(pltpu.make_async_copy(made.at[low:high], out.at[low:high], out_sems.at[i]))
        written[-1].start()
    for copy in written:
        copy.wait()


def attend(early, rows, codes, mine, theirs, other, local, raw, made):
    operands = (codes, mine, theirs, other, local, raw, made)
    state = pltpu.VMEM((2 * other.shape[1] * HDIM + codes.shape[0], HDIM), bf16)
    anywhere = pl.BlockSpec(memory_space=pl.ANY)
    return pl.pallas_call(
        functools.partial(attend_kernel, early, rows),
        out_shape=spec(*made.shape),
        in_specs=[anywhere] * 7,
        out_specs=anywhere,
        scratch_shapes=[pltpu.VMEM(a.shape, a.dtype) for a in operands]
        + [state, state, pltpu.SemaphoreType.DMA((9,)), pltpu.SemaphoreType.DMA((2,))],
        compiler_params=pltpu.CompilerParams(vmem_limit_bytes=VMEM_ALL),
        cost_estimate=LIGHT,
        name="attend",
    )(*operands)


OWN_STEPS = 4


def own_kernel(done, wq, wk, wv, out, w, sems):
    y = lax.axis_index("head")
    cols, width = w.shape[1:]
    part = cols // OWN_STEPS
    pairs = []
    for step in range(OWN_STEPS):
        begins = pl.multiple_of(y * cols + step * part, part)
        pairs += [(ref.at[pl.ds(begins, part)], w.at[i, pl.ds(step * part, part)]) for i, ref in enumerate((wq, wk, wv))]
    copies = fetch(pairs, sems)
    for step in range(OWN_STEPS):
        for copy in copies[3 * step : 3 * step + 3]:
            copy.wait()
        here = slice(step * part, (step + 1) * part)
        total = None
        for i in range(3):
            term = nt(done[:, i * width : (i + 1) * width], w[i, here])
            total = term if total is None else total + term
        out[:, here] = total.astype(bf16)


def project_own(done, weights):
    rows = done.shape[0]
    cols, width = weights[0].shape[0] // 4, weights[0].shape[1]
    return pl.pallas_call(
        own_kernel,
        out_shape=spec(rows, cols),
        in_specs=whole(1) + [pl.BlockSpec(memory_space=pl.ANY)] * 3,
        out_specs=pl.BlockSpec(memory_space=pltpu.VMEM),
        scratch_shapes=[pltpu.VMEM((3, cols, width), bf16), pltpu.SemaphoreType.DMA((3 * OWN_STEPS,))],
        compiler_params=params(),
        cost_estimate=LIGHT,
        name="project_own",
    )(done, *weights)


def arrange_kernel(*refs):
    *blocks, out = refs
    z, x, c = spot()
    outer = jnp.where(c == 0, z, x)
    share = blocks[0].shape[1]
    for far, block in enumerate(blocks):
        at = pl.multiple_of(lax.rem(outer + 4 - far, 4) * share, share)
        for src in range(3):
            out[src, pl.ds(at, share)] = block[src]


def arrange(blocks):
    srcs, share, depth = blocks[0].shape
    return pl.pallas_call(
        arrange_kernel,
        out_shape=spec(srcs, 4 * share, depth),
        in_specs=whole(4),
        out_specs=pl.BlockSpec(memory_space=pltpu.VMEM),
        compiler_params=params(),
        cost_estimate=LIGHT,
        name="arrange",
    )(*blocks)


def column_tiles(tables, cores):
    z, x, c = spot()
    for table, mirrored in zip(tables, cores):
        core = 1 - c if mirrored else c
        half = table.shape[1]
        for start in range(0, half, BLK):
            yield table, slice(start, start + BLK), pl.ds(pl.multiple_of(core * half + start, BLK), BLK)


def others_kernel(spans, cores, *refs):
    z, x, c = spot()
    parts, refs = refs[: len(spans)], refs[len(spans) :]
    tables, (partial, out) = refs[: len(cores)], refs[len(cores) :]
    for table, inside, at in column_tiles(tables, cores):
        total = partial[:, at].astype(f32)
        for (src, _), part in zip(spans, parts):
            total = total + nt(part[...], table[jnp.where(c == 1, src - 1, 2 - src), inside])
        out[:, at] = total.astype(bf16)


def project_others(parts, tables, mirrored, partial):
    spans = tuple(part[:2] for part in parts)
    operands = [*[part[2] for part in parts], *tables, partial]
    return pl.pallas_call(
        functools.partial(others_kernel, spans, mirrored),
        out_shape=spec(*partial.shape),
        in_specs=whole(len(operands)),
        out_specs=pl.BlockSpec(memory_space=pltpu.VMEM),
        input_output_aliases={len(operands) - 1: 0},
        compiler_params=params(),
        cost_estimate=LIGHT,
        name="project_others",
    )(*operands)


def last_kernel(spans, cores, *refs):
    parts, refs = refs[: len(spans)], refs[len(spans) :]
    tables, refs = refs[: len(cores)], refs[len(cores) :]
    partial, refs = refs[0], refs[1:]
    out, tiles, sems = refs[-3:]
    made = []
    for i, ((src, start), part) in enumerate(zip(spans, parts)):
        rows = part.shape[0]
        for table, inside, at in column_tiles(tables, cores):
            total = partial[start : start + rows, at].astype(f32) + nt(part[...], table[src - 1, inside])
            slot = len(made)
            tiles[slot] = total.astype(bf16)
            made.append(pltpu.make_async_copy(tiles.at[slot], out.at[pl.ds(start, rows), at], sems.at[slot]))
            made[-1].start()
    for copy in made:
        copy.wait()


def project_last(parts, tables, mirrored, partial, held=None):
    rows = parts[0][2].shape[0]
    count = len(parts) * len(tables) * tables[0].shape[1] // BLK
    spans = tuple(part[:2] for part in parts)
    operands = [*[part[2] for part in parts], *tables, partial] + ([] if held is None else [held])
    anywhere = pl.BlockSpec(memory_space=pl.ANY)
    return pl.pallas_call(
        functools.partial(last_kernel, spans, mirrored),
        out_shape=spec(*partial.shape),
        in_specs=whole(len(parts) + len(tables) + 1) + ([] if held is None else [anywhere]),
        out_specs=anywhere,
        scratch_shapes=[pltpu.VMEM((count, rows, BLK), bf16), pltpu.SemaphoreType.DMA((count,))],
        input_output_aliases={} if held is None else {len(operands) - 1: 0},
        compiler_params=params(),
        cost_estimate=LIGHT,
        name="project_last",
    )(*operands)


def turn(a, by):
    return lax.ppermute(a, "head", [(i, (i + by) % 4) for i in range(4)])


def swing(a, by):
    pairs = []
    for seq in range(32):
        for y in range(4):
            to = (y + (by if seq % 2 == 1 else -by)) % 4
            pairs.append((seq * 4 + y, seq * 4 + to))
    return lax.ppermute(a, ("seq", "head"), pairs)


def move(a, where):
    pairs = [(place(z, x, c), place(*where(z, x, c))) for z in range(4) for x in range(4) for c in range(2)]
    return lax.ppermute(a, "seq", pairs)


def across(a):
    return move(a, lambda z, x, c: (z, x, 1 - c))


CHIPS = [[place(z, x, c) for z in range(4) for x in range(4)] for c in range(2)]
def major(a, by):
    return move(a, lambda z, x, c: (z + by, x, c) if c == 0 else (z, x + by, c))


def tie(*groups):
    return lax.optimization_barrier(groups)


def shards(queries, key_rows, value_rows, grad_out, accepted, decay_code, w_query, w_key, w_value):
    heads = decay_code.shape[0]
    count = queries.shape[0]
    rows = float(count)
    weights = (w_query, w_key, w_value)
    raw, codes, local, message, *sent = begin(
        queries, key_rows, value_rows, grad_out, accepted, decay_code, weights, EARLY
    )
    other = across(message)
    leaving = join(rows, codes, message, other)
    share = [turn(sent[0], 1), turn(sent[1], -1), turn(sent[2], 2)]
    arrived = lax.all_to_all(leaving, "seq", 0, 0, axis_index_groups=CHIPS)
    held, leaving = tie((codes, raw), leaving)
    arrived, made = tie(arrived, inside(EARLY, *held))
    chip_state = gather(rows, decay_code, arrived)
    theirs = across(chip_state)
    done = attend(EARLY, rows, codes, chip_state, theirs, other, local, raw, made)
    done, *share = tie(done, *share)
    former, latter = swing(done, 1), swing(done, -1)
    total = project_own(done, weights)
    former, latter, total = tie(former, latter, total)
    share = jnp.stack(share)
    half = [share] + [major(share, by) for by in (1, 2, 3)]
    half, _, _ = tie(half, former, latter)
    half = arrange(half)
    other_half = across(half)
    far = []
    for start in range(0, count // 2, CHUNK):
        far.append((3, start, swing(former[start : start + CHUNK], 1)))
        start += count // 2
        far.append((3, start, swing(latter[start : start + CHUNK], -1)))
    sides = (1, 0, former), (2, 0, latter)
    total = project_others(sides, (half,), (False,), total)
    total = project_others(sides, (other_half,), (True,), total)
    out = None
    for i in range(0, len(far), 2):
        out = project_last(far[i : i + 2], (half, other_half), (False, True), total, out)
    return out


def solution(mesh):
    in_specs = (P("seq", "head"),) * 4 + (P("seq"), P("head")) + (P(None, "head"),) * 3
    return jax.shard_map(shards, mesh=mesh, in_specs=in_specs, out_specs=P("seq", "head"), check_vma=False)
```

```python
import functools

import jax
import jax.numpy as jnp
from jax import lax
from jax.experimental import pallas as pl
from jax.experimental.pallas import tpu as pltpu
from jax.sharding import PartitionSpec as P

BLK = 256
EARLY = 512
CHUNK = 256
HDIM = 128
bf16 = jnp.bfloat16
f32 = jnp.float32
VMEM_LIMIT = 24 * 1024 * 1024
VMEM_ALL = 62 * 1024 * 1024
LIGHT = pl.CostEstimate(flops=1, bytes_accessed=1, transcendentals=0)

SHARES = 8


def place(z, x, c):
    return (z % 4) * 8 + (x % 4) * 2 + c % 2


def nt(a, b):
    return lax.dot_general(a, b, (((1,), (1,)), ((), ())), preferred_element_type=f32)


def nn(a, b):
    return lax.dot_general(a, b, (((1,), (0,)), ((), ())), preferred_element_type=f32)


def tn(a, b):
    return lax.dot_general(a, b, (((0,), (0,)), ((), ())), preferred_element_type=f32)


def spec(*shape):
    return jax.ShapeDtypeStruct(shape, bf16)


def params():
    return pltpu.CompilerParams(vmem_limit_bytes=VMEM_LIMIT)


def whole(count):
    return [pl.BlockSpec(memory_space=pltpu.VMEM)] * count


def fetch(pairs, sems):
    copies = [pltpu.make_async_copy(source, target, sems.at[i]) for i, (source, target) in enumerate(pairs)]
    for copy in copies:
        copy.start()
    return copies


def begin_kernel(
    cut, q, k, v, g, accepted, decay_code, wq, wk, wv, raw, codes, local, message, s1, s2, s3, raw_g, keep, sems
):
    width = q.shape[1]
    rows = raw.shape[0]
    pairs = [(g, raw_g), (accepted, keep)]
    for part, ref in enumerate((q, k, v)):
        pairs.append((ref, raw.at[:, pl.ds(part * width, width)]))
    y = lax.axis_index("head")
    z, x, c = spot()
    piece = c * 4 + jnp.where(c == 0, z, x)
    for out, by in zip((s1, s2, s3), (1, 3, 2)):
        for part, w in enumerate((wq, wk, wv)):
            pairs.append((w.at[lax.rem(y + by, 4), piece], out.at[:, pl.ds(part * width, width)]))
    copies = fetch(pairs, sems)
    line = lax.broadcasted_iota(jnp.int32, codes.shape, 0)
    filled = jnp.zeros(codes.shape, f32)
    for head in range(decay_code.shape[0]):
        filled = jnp.where(line == head, decay_code[head].astype(f32), filled)
    codes[...] = filled.astype(bf16)
    for copy in copies[:2]:
        copy.wait()
    column = jnp.broadcast_to(keep[0:1, :].astype(f32), (HDIM, rows)).T
    wide = jnp.concatenate([column] * (width // HDIM), axis=1)
    raw[:, 3 * width :] = (raw_g[...].astype(f32) * wide).astype(bf16)
    for copy in copies[2:]:
        copy.wait()
    for head in range(local.shape[2]):
        rate = jnp.exp2(-0.5 * jnp.full((1, HDIM), decay_code[head], f32))
        found, spans = [], []
        for half, (low, high) in enumerate(((0, cut), (cut, rows))):
            where = lax.broadcasted_iota(jnp.int32, (high - low, HDIM), 0).astype(f32)
            to_end = jnp.exp(-rate * (high - low - 1.0 - where))
            from_start = jnp.exp(-rate * where)
            spans.append(jnp.exp(-rate * (high - low)))
            at = lambda part: raw[low:high, part * width + head * HDIM : part * width + (head + 1) * HDIM]
            kv = tn((at(1).astype(f32) * to_end).astype(bf16), at(2))
            qg = tn((at(0).astype(f32) * from_start).astype(bf16), at(3))
            found.append((kv, qg))
            local[half, 0, head] = kv
            local[half, 1, head] = qg
        message[0, head] = (spans[1] * found[0][0] + found[1][0]).astype(bf16)
        message[1, head] = (found[0][1] + spans[0] * found[1][1]).astype(bf16)


def begin(q, k, v, g, accepted, decay_code, weights, early):
    rows, width = q.shape
    out_rows = weights[0].shape[0]
    share = out_rows // (4 * SHARES)
    shaped = [w.reshape(4, SHARES, share, width) for w in weights]
    heads = decay_code.shape[0]
    far = pl.BlockSpec(memory_space=pl.ANY)
    return pl.pallas_call(
        functools.partial(begin_kernel, early),
        out_shape=[
            spec(rows, 4 * width),
            spec(16, HDIM),
            jax.ShapeDtypeStruct((2, 2, heads, HDIM, HDIM), f32),
            spec(2, heads, HDIM, HDIM),
            *[spec(share, 3 * width)] * 3,
        ],
        in_specs=[far] * 5 + [pl.BlockSpec(memory_space=pltpu.SMEM)] + [far] * 3,
        out_specs=whole(7),
        scratch_shapes=[
            pltpu.VMEM((rows, width), bf16),
            pltpu.VMEM((1, rows), jnp.int32),
            pltpu.SemaphoreType.DMA((14,)),
        ],
        compiler_params=pltpu.CompilerParams(vmem_limit_bytes=VMEM_ALL),
        cost_estimate=LIGHT,
        name="begin",
    )(q, k, v, g, accepted.reshape(1, rows), decay_code, *shaped)


def spot():
    seq = lax.axis_index("seq")
    return lax.div(seq, 8), lax.rem(lax.div(seq, 2), 4), lax.rem(seq, 2)


def fade(codes, head, span, count):
    rate = jnp.exp2(-0.5 * codes[head : head + 1, :].astype(f32))
    faded = jnp.exp(-rate * (span * jnp.maximum(count, 0).astype(f32)))
    return jnp.where(count >= 0, faded, 0.0)


def join_kernel(rows, codes_at, mine_at, other_at, out, codes, mine, other, sems):
    z, x, c = spot()
    late = c == 1
    chip = z * 4 + x
    for copy in fetch([(codes_at, codes), (mine_at, mine), (other_at, other)], sems):
        copy.wait()
    for head in range(mine.shape[1]):
        one = fade(codes, head, rows, jnp.int32(1))
        near, far = mine[:, head].astype(f32), other[:, head].astype(f32)
        before, after = jnp.where(late, far, near), jnp.where(late, near, far)
        kv = (one * before[0] + after[0]).astype(bf16)
        qg = (before[1] + one * after[1]).astype(bf16)
        for to in range(out.shape[0]):

            @pl.when(c == head)
            def _(to=to, kv=kv, qg=qg):
                out[to, 0] = jnp.where(to > chip, kv, qg)


def join(rows, codes, mine, other):
    return pl.pallas_call(
        functools.partial(join_kernel, rows),
        out_shape=spec(16, 1, *mine.shape[2:]),
        in_specs=[pl.BlockSpec(memory_space=pl.ANY)] * 3,
        out_specs=pl.BlockSpec(memory_space=pltpu.VMEM),
        scratch_shapes=[
            pltpu.VMEM(codes.shape, bf16),
            pltpu.VMEM(mine.shape, bf16),
            pltpu.VMEM(other.shape, bf16),
            pltpu.SemaphoreType.DMA((3,)),
        ],
        compiler_params=pltpu.CompilerParams(vmem_limit_bytes=VMEM_ALL),
        cost_estimate=LIGHT,
        name="join",
    )(codes, mine, other)


def gather_kernel(rows, decay_code, arrived, out):
    z, x, c = spot()
    chip = z * 4 + x
    kv = qg = jnp.zeros((HDIM, HDIM), f32)
    code = jnp.full((1, HDIM), jnp.where(c == 0, decay_code[0], decay_code[1]), jnp.int32)
    for there in range(arrived.shape[0]):
        it = arrived[there, 0].astype(f32)
        kv += it * fade(code, 0, 2 * rows, chip - 1 - there)
        qg += it * fade(code, 0, 2 * rows, there - chip - 1)
    out[0] = kv.astype(bf16)
    out[1] = qg.astype(bf16)


def enter_states(early, rows, codes, mine, theirs, other, local, state0, state1):
    z, x, c = spot()
    late = c == 1
    heads = other.shape[1]
    width = heads * HDIM
    for head in range(heads):
        kv = jnp.where(c == head, mine[0], theirs[0]).astype(f32)
        qg = jnp.where(c == head, mine[1], theirs[1]).astype(f32)
        one = fade(codes, head, rows, jnp.int32(1))
        start = fade(codes, head, early, jnp.int32(1))
        end = fade(codes, head, rows - early, jnp.int32(1))
        kv = jnp.where(late, one * kv + other[0, head].astype(f32), kv)
        qg = jnp.where(late, qg, one * qg + other[1, head].astype(f32))
        here = pl.ds(head * HDIM, HDIM)
        there = pl.ds(width + head * HDIM, HDIM)
        state0[here] = kv.astype(bf16)
        state0[there] = (end * qg + local[1, 1, head]).astype(bf16)
        state1[here] = (start * kv + local[0, 0, head]).astype(bf16)
        state1[there] = qg.astype(bf16)
    state0[2 * width :] = codes[...]
    state1[2 * width :] = codes[...]


def gather(rows, decay_code, arrived):
    return pl.pallas_call(
        functools.partial(gather_kernel, rows),
        out_shape=spec(2, HDIM, HDIM),
        in_specs=[pl.BlockSpec(memory_space=pltpu.SMEM), pl.BlockSpec(memory_space=pltpu.VMEM)],
        out_specs=pl.BlockSpec(memory_space=pltpu.VMEM),
        compiler_params=params(),
        cost_estimate=LIGHT,
        name="gather",
    )(decay_code, arrived)


def attend_rows(raws, codes, out_rows, first_row, targets):
    width = raws[0].shape[1] // 4
    heads = width // HDIM
    rows = out_rows
    starts = list(range(0, rows, BLK))
    sizes = [min(BLK, rows - start) for start in starts]
    count = len(starts)
    edges = [0]
    for raw in raws:
        edges.append(edges[-1] + raw.shape[0])

    def take(block, part, head):
        low, high = starts[block], starts[block] + sizes[block]
        here = slice(part * width + head * HDIM, part * width + (head + 1) * HDIM)
        found = []
        for raw, start, end in zip(raws, edges, edges[1:]):
            if max(low, start) < min(high, end):
                found.append(raw[max(low, start) - start : min(high, end) - start, here])
        return found[0] if len(found) == 1 else jnp.concatenate(found, axis=0)

    def table(rate1, later, earlier, flip):
        shape = (sizes[earlier], sizes[later]) if flip else (sizes[later], sizes[earlier])
        row = lax.broadcasted_iota(jnp.int32, shape, 0)
        col = lax.broadcasted_iota(jnp.int32, shape, 1)
        rate = rate1 if shape[1] == HDIM else jnp.concatenate([rate1] * (shape[1] // HDIM), axis=1)
        gap = (col - row if flip else row - col).astype(f32)
        if later == earlier:
            return jnp.where(gap >= 0, jnp.exp(-rate * jnp.maximum(gap, 0.0)), 0.0)
        return jnp.exp(-rate * (starts[later] - starts[earlier] + gap))

    cut = lambda a, d: (a * d).astype(bf16)
    for head in range(heads):
        rate = jnp.exp2(-0.5 * codes[head : head + 1, :].astype(f32))
        made = {}

        def decay(later, earlier, flip):
            key = (starts[later] - starts[earlier], sizes[later], sizes[earlier], flip)
            if key not in made:
                made[key] = table(rate, later, earlier, flip)
            return made[key]

        q, k, v, g = ([take(block, part, head) for block in range(count)] for part in range(4))
        for block in range(count):
            start, size = starts[block], sizes[block]
            dq = dk = dv = jnp.zeros((size, HDIM), f32)
            for other in range(block + 1):
                dq += nn(cut(nt(g[block], v[other]), decay(block, other, False)), k[other])
            for other in range(block, count):
                dk += nn(cut(nt(v[block], g[other]), decay(other, block, True)), q[other])
                dv += nn(cut(nt(k[block], q[other]), decay(other, block, True)), g[other])
            for part, value in enumerate((dq, dk, dv)):
                here = pl.ds(part * width + head * HDIM, HDIM)
                value = value.astype(bf16)
                low = first_row + start
                for ref, begins in targets:
                    from_row, to_row = max(low, begins), min(low + size, begins + ref.shape[0])
                    if from_row < to_row:
                        ref[from_row - begins : to_row - begins, here] = value[from_row - low : to_row - low]


def inside_kernel(early, codes_at, raw_at, out, codes, raw, made, sems, out_sems):
    copies = fetch([(codes_at, codes), (raw_at, raw)], sems)
    for copy in copies:
        copy.wait()
    count = made.shape[0]
    written = []
    for i, (low, high) in enumerate(((0, early), (early, count))):
        attend_rows([raw.at[low:high]], codes, high - low, low, [(made, 0)])
        written.append(pltpu.make_async_copy(made.at[low:high], out.at[low:high], out_sems.at[i]))
        written[-1].start()
    for copy in written:
        copy.wait()


def inside(early, codes, raw):
    count, depth = raw.shape[0], raw.shape[1] // 4 * 3
    anywhere = pl.BlockSpec(memory_space=pl.ANY)
    return pl.pallas_call(
        functools.partial(inside_kernel, early),
        out_shape=spec(count, depth),
        in_specs=[anywhere] * 2,
        out_specs=anywhere,
        scratch_shapes=[
            pltpu.VMEM(codes.shape, bf16),
            pltpu.VMEM(raw.shape, bf16),
            pltpu.VMEM((count, depth), bf16),
            pltpu.SemaphoreType.DMA((2,)),
            pltpu.SemaphoreType.DMA((2,)),
        ],
        compiler_params=pltpu.CompilerParams(vmem_limit_bytes=VMEM_ALL),
        cost_estimate=LIGHT,
        name="inside",
    )(codes, raw)


def attend_kernel(early, rows, *refs):
    inputs, out, rest = refs[:7], refs[7], refs[8:]
    held, (state0, state1, sems, out_sems) = rest[:7], rest[7:]
    pairs = list(zip(inputs[:5], held[:5]))
    count = held[6].shape[0]
    for low in range(0, count, BLK):
        part = slice(low, low + BLK)
        pairs += [(source.at[part], target.at[part]) for source, target in zip(inputs[5:], held[5:])]
    copies = fetch(pairs, sems)
    for copy in copies[:5]:
        copy.wait()
    codes, raw, made = held[0], held[5], held[6]
    width = made.shape[1] // 3
    enter_states(float(early), rows, *held[:5], state0, state1)
    written = []
    for i, low in enumerate(range(0, count, BLK)):
        high = low + BLK
        begins, ends, state = (0, early, state0) if high <= early else (early, count, state1)
        for copy in copies[5 + 2 * i : 7 + 2 * i]:
            copy.wait()
        where = lax.broadcasted_iota(jnp.int32, (BLK, HDIM), 0).astype(f32) + (low - begins)
        for head in range(width // HDIM):
            rate = jnp.exp2(-0.5 * codes[head : head + 1, :].astype(f32))
            lead, lag = jnp.exp(-rate * (where + 1.0)), jnp.exp(-rate * (ends - begins - where))
            k, v, g = (raw[low:high, part * width + head * HDIM : part * width + (head + 1) * HDIM] for part in (1, 2, 3))
            kv = state[head * HDIM : (head + 1) * HDIM, :]
            qg = state[width + head * HDIM : width + (head + 1) * HDIM, :]
            for part, value in enumerate((lead * nt(g, kv), lag * nt(v, qg), lag * nn(k, qg))):
                here = pl.ds(part * width + head * HDIM, HDIM)
                made[low:high, here] = (made[low:high, here].astype(f32) + value).astype(bf16)
        written.append(pltpu.make_async_copy(made.at[low:high], out.at[low:high], out_sems.at[i]))
        written[-1].start()
    for copy in written:
        copy.wait()


def attend(early, rows, codes, mine, theirs, other, local, raw, made):
    operands = (codes, mine, theirs, other, local, raw, made)
    state = pltpu.VMEM((2 * other.shape[1] * HDIM + codes.shape[0], HDIM), bf16)
    anywhere = pl.BlockSpec(memory_space=pl.ANY)
    return pl.pallas_call(
        functools.partial(attend_kernel, early, rows),
        out_shape=spec(*made.shape),
        in_specs=[anywhere] * 7,
        out_specs=anywhere,
        scratch_shapes=[pltpu.VMEM(a.shape, a.dtype) for a in operands]
        + [state, state, pltpu.SemaphoreType.DMA((5 + 2 * (made.shape[0] // BLK),)), pltpu.SemaphoreType.DMA((made.shape[0] // BLK,))],
        compiler_params=pltpu.CompilerParams(vmem_limit_bytes=VMEM_ALL),
        cost_estimate=LIGHT,
        name="attend",
    )(*operands)


OWN_STEPS = 4


def own_kernel(done, wq, wk, wv, out, w, sems):
    y = lax.axis_index("head")
    cols, width = w.shape[1:]
    part = cols // OWN_STEPS
    pairs = []
    for step in range(OWN_STEPS):
        begins = pl.multiple_of(y * cols + step * part, part)
        pairs += [(ref.at[pl.ds(begins, part)], w.at[i, pl.ds(step * part, part)]) for i, ref in enumerate((wq, wk, wv))]
    copies = fetch(pairs, sems)
    for step in range(OWN_STEPS):
        for copy in copies[3 * step : 3 * step + 3]:
            copy.wait()
        here = slice(step * part, (step + 1) * part)
        total = None
        for i in range(3):
            term = nt(done[:, i * width : (i + 1) * width], w[i, here])
            total = term if total is None else total + term
        out[:, here] = total.astype(bf16)


def project_own(done, weights):
    rows = done.shape[0]
    cols, width = weights[0].shape[0] // 4, weights[0].shape[1]
    return pl.pallas_call(
        own_kernel,
        out_shape=spec(rows, cols),
        in_specs=whole(1) + [pl.BlockSpec(memory_space=pl.ANY)] * 3,
        out_specs=pl.BlockSpec(memory_space=pltpu.VMEM),
        scratch_shapes=[pltpu.VMEM((3, cols, width), bf16), pltpu.SemaphoreType.DMA((3 * OWN_STEPS,))],
        compiler_params=params(),
        cost_estimate=LIGHT,
        name="project_own",
    )(done, *weights)


def arrange_kernel(*refs):
    *blocks, out = refs
    z, x, c = spot()
    outer = jnp.where(c == 0, z, x)
    share = blocks[0].shape[1]
    for far, block in enumerate(blocks):
        at = pl.multiple_of(lax.rem(outer + 4 - far, 4) * share, share)
        for src in range(3):
            out[src, pl.ds(at, share)] = block[src]


def arrange(blocks):
    srcs, share, depth = blocks[0].shape
    return pl.pallas_call(
        arrange_kernel,
        out_shape=spec(srcs, 4 * share, depth),
        in_specs=whole(4),
        out_specs=pl.BlockSpec(memory_space=pltpu.VMEM),
        compiler_params=params(),
        cost_estimate=LIGHT,
        name="arrange",
    )(*blocks)


def column_tiles(tables, cores):
    z, x, c = spot()
    for table, mirrored in zip(tables, cores):
        core = 1 - c if mirrored else c
        half = table.shape[1]
        for start in range(0, half, BLK):
            yield table, slice(start, start + BLK), pl.ds(pl.multiple_of(core * half + start, BLK), BLK)


def others_kernel(spans, cores, *refs):
    z, x, c = spot()
    parts, refs = refs[: len(spans)], refs[len(spans) :]
    tables, (partial, out) = refs[: len(cores)], refs[len(cores) :]
    for table, inside, at in column_tiles(tables, cores):
        total = partial[:, at].astype(f32)
        for (src, _), part in zip(spans, parts):
            total = total + nt(part[...], table[jnp.where(c == 1, src - 1, 2 - src), inside])
        out[:, at] = total.astype(bf16)


def project_others(parts, tables, mirrored, partial):
    spans = tuple(part[:2] for part in parts)
    operands = [*[part[2] for part in parts], *tables, partial]
    return pl.pallas_call(
        functools.partial(others_kernel, spans, mirrored),
        out_shape=spec(*partial.shape),
        in_specs=whole(len(operands)),
        out_specs=pl.BlockSpec(memory_space=pltpu.VMEM),
        input_output_aliases={len(operands) - 1: 0},
        compiler_params=params(),
        cost_estimate=LIGHT,
        name="project_others",
    )(*operands)


def last_kernel(spans, cores, *refs):
    parts, refs = refs[: len(spans)], refs[len(spans) :]
    tables, refs = refs[: len(cores)], refs[len(cores) :]
    partial, refs = refs[0], refs[1:]
    out, tiles, sems = refs[-3:]
    made = []
    for i, ((src, start), part) in enumerate(zip(spans, parts)):
        rows = part.shape[0]
        for table, inside, at in column_tiles(tables, cores):
            total = partial[start : start + rows, at].astype(f32) + nt(part[...], table[src - 1, inside])
            slot = len(made)
            tiles[slot] = total.astype(bf16)
            made.append(pltpu.make_async_copy(tiles.at[slot], out.at[pl.ds(start, rows), at], sems.at[slot]))
            made[-1].start()
    for copy in made:
        copy.wait()


def project_last(parts, tables, mirrored, partial, held=None):
    rows = parts[0][2].shape[0]
    count = len(parts) * len(tables) * tables[0].shape[1] // BLK
    spans = tuple(part[:2] for part in parts)
    operands = [*[part[2] for part in parts], *tables, partial] + ([] if held is None else [held])
    anywhere = pl.BlockSpec(memory_space=pl.ANY)
    return pl.pallas_call(
        functools.partial(last_kernel, spans, mirrored),
        out_shape=spec(*partial.shape),
        in_specs=whole(len(parts) + len(tables) + 1) + ([] if held is None else [anywhere]),
        out_specs=anywhere,
        scratch_shapes=[pltpu.VMEM((count, rows, BLK), bf16), pltpu.SemaphoreType.DMA((count,))],
        input_output_aliases={} if held is None else {len(operands) - 1: 0},
        compiler_params=params(),
        cost_estimate=LIGHT,
        name="project_last",
    )(*operands)


def turn(a, by):
    return lax.ppermute(a, "head", [(i, (i + by) % 4) for i in range(4)])


def swing(a, by):
    pairs = []
    for seq in range(32):
        for y in range(4):
            to = (y + (by if seq % 2 == 1 else -by)) % 4
            pairs.append((seq * 4 + y, seq * 4 + to))
    return lax.ppermute(a, ("seq", "head"), pairs)


def move(a, where):
    pairs = [(place(z, x, c), place(*where(z, x, c))) for z in range(4) for x in range(4) for c in range(2)]
    return lax.ppermute(a, "seq", pairs)


def across(a):
    return move(a, lambda z, x, c: (z, x, 1 - c))


CHIPS = [[place(z, x, c) for z in range(4) for x in range(4)] for c in range(2)]
def major(a, by):
    return move(a, lambda z, x, c: (z + by, x, c) if c == 0 else (z, x + by, c))


def tie(*groups):
    return lax.optimization_barrier(groups)


def shards(queries, key_rows, value_rows, grad_out, accepted, decay_code, w_query, w_key, w_value):
    heads = decay_code.shape[0]
    count = queries.shape[0]
    rows = float(count)
    weights = (w_query, w_key, w_value)
    raw, codes, local, message, *sent = begin(
        queries, key_rows, value_rows, grad_out, accepted, decay_code, weights, EARLY
    )
    other = across(message)
    leaving = join(rows, codes, message, other)
    share = [turn(sent[0], 1), turn(sent[1], -1), turn(sent[2], 2)]
    arrived = lax.all_to_all(leaving, "seq", 0, 0, axis_index_groups=CHIPS)
    held, leaving = tie((codes, raw), leaving)
    arrived, made = tie(arrived, inside(EARLY, *held))
    chip_state = gather(rows, decay_code, arrived)
    theirs = across(chip_state)
    done = attend(EARLY, rows, codes, chip_state, theirs, other, local, raw, made)
    done, *share = tie(done, *share)
    former, latter = swing(done, 1), swing(done, -1)
    total = project_own(done, weights)
    former, latter, total = tie(former, latter, total)
    share = jnp.stack(share)
    half = [share] + [major(share, by) for by in (1, 2, 3)]
    half, _, _ = tie(half, former, latter)
    half = arrange(half)
    other_half = across(half)
    far = []
    for start in range(0, count // 2, CHUNK):
        far.append((3, start, swing(former[start : start + CHUNK], 1)))
        start += count // 2
        far.append((3, start, swing(latter[start : start + CHUNK], -1)))
    sides = (1, 0, former), (2, 0, latter)
    total = project_others(sides, (half,), (False,), total)
    total = project_others(sides, (other_half,), (True,), total)
    out = None
    for i in range(0, len(far), 2):
        out = project_last(far[i : i + 2], (half, other_half), (False, True), total, out)
    return out


def solution(mesh):
    in_specs = (P("seq", "head"),) * 4 + (P("seq"), P("head")) + (P(None, "head"),) * 3
    return jax.shard_map(shards, mesh=mesh, in_specs=in_specs, out_specs=P("seq", "head"), check_vma=False)
```

```python
import functools

import jax
import jax.numpy as jnp
from jax import lax
from jax.experimental import pallas as pl
from jax.experimental.pallas import tpu as pltpu
from jax.sharding import PartitionSpec as P

BLK = 256
EARLY = 512
CHUNK = 256
HDIM = 128
bf16 = jnp.bfloat16
f32 = jnp.float32
VMEM_LIMIT = 24 * 1024 * 1024
VMEM_ALL = 62 * 1024 * 1024
LIGHT = pl.CostEstimate(flops=1, bytes_accessed=1, transcendentals=0)

SHARES = 8


def place(z, x, c):
    return (z % 4) * 8 + (x % 4) * 2 + c % 2


def nt(a, b):
    return lax.dot_general(a, b, (((1,), (1,)), ((), ())), preferred_element_type=f32)


def nn(a, b):
    return lax.dot_general(a, b, (((1,), (0,)), ((), ())), preferred_element_type=f32)


def tn(a, b):
    return lax.dot_general(a, b, (((0,), (0,)), ((), ())), preferred_element_type=f32)


def spec(*shape):
    return jax.ShapeDtypeStruct(shape, bf16)


def params():
    return pltpu.CompilerParams(vmem_limit_bytes=VMEM_LIMIT)


def whole(count):
    return [pl.BlockSpec(memory_space=pltpu.VMEM)] * count


def fetch(pairs, sems):
    copies = [pltpu.make_async_copy(source, target, sems.at[i]) for i, (source, target) in enumerate(pairs)]
    for copy in copies:
        copy.start()
    return copies


def begin_kernel(
    cut, q, k, v, g, accepted, decay_code, wq, wk, wv, raw, codes, local, message, s1, s2, s3, raw_g, keep, sems
):
    width = q.shape[1]
    rows = raw.shape[0]
    pairs = [(g, raw_g), (accepted, keep)]
    for part, ref in enumerate((q, k, v)):
        pairs.append((ref, raw.at[:, pl.ds(part * width, width)]))
    y = lax.axis_index("head")
    z, x, c = spot()
    piece = c * 4 + jnp.where(c == 0, z, x)
    for out, by in zip((s1, s2, s3), (1, 3, 2)):
        for part, w in enumerate((wq, wk, wv)):
            pairs.append((w.at[lax.rem(y + by, 4), piece], out.at[:, pl.ds(part * width, width)]))
    copies = fetch(pairs, sems)
    line = lax.broadcasted_iota(jnp.int32, codes.shape, 0)
    filled = jnp.zeros(codes.shape, f32)
    for head in range(decay_code.shape[0]):
        filled = jnp.where(line == head, decay_code[head].astype(f32), filled)
    codes[...] = filled.astype(bf16)
    for copy in copies[:2]:
        copy.wait()
    column = jnp.broadcast_to(keep[0:1, :].astype(f32), (HDIM, rows)).T
    wide = jnp.concatenate([column] * (width // HDIM), axis=1)
    raw[:, 3 * width :] = (raw_g[...].astype(f32) * wide).astype(bf16)
    for copy in copies[2:]:
        copy.wait()
    for head in range(local.shape[2]):
        rate = jnp.exp2(-0.5 * jnp.full((1, HDIM), decay_code[head], f32))
        found, spans = [], []
        for half, (low, high) in enumerate(((0, cut), (cut, rows))):
            where = lax.broadcasted_iota(jnp.int32, (high - low, HDIM), 0).astype(f32)
            to_end = jnp.exp(-rate * (high - low - 1.0 - where))
            from_start = jnp.exp(-rate * where)
            spans.append(jnp.exp(-rate * (high - low)))
            at = lambda part: raw[low:high, part * width + head * HDIM : part * width + (head + 1) * HDIM]
            kv = tn((at(1).astype(f32) * to_end).astype(bf16), at(2))
            qg = tn((at(0).astype(f32) * from_start).astype(bf16), at(3))
            found.append((kv, qg))
            local[half, 0, head] = kv
            local[half, 1, head] = qg
        message[0, head] = (spans[1] * found[0][0] + found[1][0]).astype(bf16)
        message[1, head] = (found[0][1] + spans[0] * found[1][1]).astype(bf16)


def begin(q, k, v, g, accepted, decay_code, weights, early):
    rows, width = q.shape
    out_rows = weights[0].shape[0]
    share = out_rows // (4 * SHARES)
    shaped = [w.reshape(4, SHARES, share, width) for w in weights]
    heads = decay_code.shape[0]
    far = pl.BlockSpec(memory_space=pl.ANY)
    return pl.pallas_call(
        functools.partial(begin_kernel, early),
        out_shape=[
            spec(rows, 4 * width),
            spec(16, HDIM),
            jax.ShapeDtypeStruct((2, 2, heads, HDIM, HDIM), f32),
            spec(2, heads, HDIM, HDIM),
            *[spec(share, 3 * width)] * 3,
        ],
        in_specs=[far] * 5 + [pl.BlockSpec(memory_space=pltpu.SMEM)] + [far] * 3,
        out_specs=whole(7),
        scratch_shapes=[
            pltpu.VMEM((rows, width), bf16),
            pltpu.VMEM((1, rows), jnp.int32),
            pltpu.SemaphoreType.DMA((14,)),
        ],
        compiler_params=pltpu.CompilerParams(vmem_limit_bytes=VMEM_ALL),
        cost_estimate=LIGHT,
        name="begin",
    )(q, k, v, g, accepted.reshape(1, rows), decay_code, *shaped)


def spot():
    seq = lax.axis_index("seq")
    return lax.div(seq, 8), lax.rem(lax.div(seq, 2), 4), lax.rem(seq, 2)


def fade(codes, head, span, count):
    rate = jnp.exp2(-0.5 * codes[head : head + 1, :].astype(f32))
    faded = jnp.exp(-rate * (span * jnp.maximum(count, 0).astype(f32)))
    return jnp.where(count >= 0, faded, 0.0)


def join_kernel(rows, codes_at, mine_at, other_at, out, codes, mine, other, sems):
    z, x, c = spot()
    late = c == 1
    chip = z * 4 + x
    for copy in fetch([(codes_at, codes), (mine_at, mine), (other_at, other)], sems):
        copy.wait()
    for head in range(mine.shape[1]):
        one = fade(codes, head, rows, jnp.int32(1))
        near, far = mine[:, head].astype(f32), other[:, head].astype(f32)
        before, after = jnp.where(late, far, near), jnp.where(late, near, far)
        kv = (one * before[0] + after[0]).astype(bf16)
        qg = (before[1] + one * after[1]).astype(bf16)
        for to in range(out.shape[0]):

            @pl.when(c == head)
            def _(to=to, kv=kv, qg=qg):
                out[to, 0] = jnp.where(to > chip, kv, qg)


def join(rows, codes, mine, other):
    return pl.pallas_call(
        functools.partial(join_kernel, rows),
        out_shape=spec(16, 1, *mine.shape[2:]),
        in_specs=[pl.BlockSpec(memory_space=pl.ANY)] * 3,
        out_specs=pl.BlockSpec(memory_space=pltpu.VMEM),
        scratch_shapes=[
            pltpu.VMEM(codes.shape, bf16),
            pltpu.VMEM(mine.shape, bf16),
            pltpu.VMEM(other.shape, bf16),
            pltpu.SemaphoreType.DMA((3,)),
        ],
        compiler_params=pltpu.CompilerParams(vmem_limit_bytes=VMEM_ALL),
        cost_estimate=LIGHT,
        name="join",
    )(codes, mine, other)


def gather_kernel(rows, decay_code, arrived, out):
    z, x, c = spot()
    chip = z * 4 + x
    kv = qg = jnp.zeros((HDIM, HDIM), f32)
    code = jnp.full((1, HDIM), jnp.where(c == 0, decay_code[0], decay_code[1]), jnp.int32)
    for there in range(arrived.shape[0]):
        it = arrived[there, 0].astype(f32)
        kv += it * fade(code, 0, 2 * rows, chip - 1 - there)
        qg += it * fade(code, 0, 2 * rows, there - chip - 1)
    out[0] = kv.astype(bf16)
    out[1] = qg.astype(bf16)


def enter_states(early, rows, codes, mine, theirs, other, local, state0, state1):
    z, x, c = spot()
    late = c == 1
    heads = other.shape[1]
    width = heads * HDIM
    for head in range(heads):
        kv = jnp.where(c == head, mine[0], theirs[0]).astype(f32)
        qg = jnp.where(c == head, mine[1], theirs[1]).astype(f32)
        one = fade(codes, head, rows, jnp.int32(1))
        start = fade(codes, head, early, jnp.int32(1))
        end = fade(codes, head, rows - early, jnp.int32(1))
        kv = jnp.where(late, one * kv + other[0, head].astype(f32), kv)
        qg = jnp.where(late, qg, one * qg + other[1, head].astype(f32))
        here = pl.ds(head * HDIM, HDIM)
        there = pl.ds(width + head * HDIM, HDIM)
        state0[here] = kv.astype(bf16)
        state0[there] = (end * qg + local[1, 1, head]).astype(bf16)
        state1[here] = (start * kv + local[0, 0, head]).astype(bf16)
        state1[there] = qg.astype(bf16)
    state0[2 * width :] = codes[...]
    state1[2 * width :] = codes[...]


def gather(rows, decay_code, arrived):
    return pl.pallas_call(
        functools.partial(gather_kernel, rows),
        out_shape=spec(2, HDIM, HDIM),
        in_specs=[pl.BlockSpec(memory_space=pltpu.SMEM), pl.BlockSpec(memory_space=pltpu.VMEM)],
        out_specs=pl.BlockSpec(memory_space=pltpu.VMEM),
        compiler_params=params(),
        cost_estimate=LIGHT,
        name="gather",
    )(decay_code, arrived)


def attend_rows(raws, codes, out_rows, first_row, targets):
    width = raws[0].shape[1] // 4
    heads = width // HDIM
    rows = out_rows
    starts = list(range(0, rows, BLK))
    sizes = [min(BLK, rows - start) for start in starts]
    count = len(starts)
    edges = [0]
    for raw in raws:
        edges.append(edges[-1] + raw.shape[0])

    def take(block, part, head):
        low, high = starts[block], starts[block] + sizes[block]
        here = slice(part * width + head * HDIM, part * width + (head + 1) * HDIM)
        found = []
        for raw, start, end in zip(raws, edges, edges[1:]):
            if max(low, start) < min(high, end):
                found.append(raw[max(low, start) - start : min(high, end) - start, here])
        return found[0] if len(found) == 1 else jnp.concatenate(found, axis=0)

    def table(rate1, later, earlier, flip):
        shape = (sizes[earlier], sizes[later]) if flip else (sizes[later], sizes[earlier])
        row = lax.broadcasted_iota(jnp.int32, shape, 0)
        col = lax.broadcasted_iota(jnp.int32, shape, 1)
        rate = rate1 if shape[1] == HDIM else jnp.concatenate([rate1] * (shape[1] // HDIM), axis=1)
        gap = (col - row if flip else row - col).astype(f32)
        if later == earlier:
            return jnp.where(gap >= 0, jnp.exp(-rate * jnp.maximum(gap, 0.0)), 0.0)
        return jnp.exp(-rate * (starts[later] - starts[earlier] + gap))

    cut = lambda a, d: (a * d).astype(bf16)
    for head in range(heads):
        rate = jnp.exp2(-0.5 * codes[head : head + 1, :].astype(f32))
        made = {}

        def decay(later, earlier, flip):
            key = (starts[later] - starts[earlier], sizes[later], sizes[earlier], flip)
            if key not in made:
                made[key] = table(rate, later, earlier, flip)
            return made[key]

        q, k, v, g = ([take(block, part, head) for block in range(count)] for part in range(4))
        for block in range(count):
            start, size = starts[block], sizes[block]
            dq = dk = dv = jnp.zeros((size, HDIM), f32)
            for other in range(block + 1):
                dq += nn(cut(nt(g[block], v[other]), decay(block, other, False)), k[other])
            for other in range(block, count):
                dk += nn(cut(nt(v[block], g[other]), decay(other, block, True)), q[other])
                dv += nn(cut(nt(k[block], q[other]), decay(other, block, True)), g[other])
            for part, value in enumerate((dq, dk, dv)):
                here = pl.ds(part * width + head * HDIM, HDIM)
                value = value.astype(bf16)
                low = first_row + start
                for ref, begins in targets:
                    from_row, to_row = max(low, begins), min(low + size, begins + ref.shape[0])
                    if from_row < to_row:
                        ref[from_row - begins : to_row - begins, here] = value[from_row - low : to_row - low]


def inside_kernel(early, codes_at, raw_at, out, codes, raw, made, sems, out_sems):
    copies = fetch([(codes_at, codes), (raw_at, raw)], sems)
    for copy in copies:
        copy.wait()
    count = made.shape[0]
    written = []
    for i, (low, high) in enumerate(((0, early), (early, count))):
        attend_rows([raw.at[low:high]], codes, high - low, low, [(made, 0)])
        written.append(pltpu.make_async_copy(made.at[low:high], out.at[low:high], out_sems.at[i]))
        written[-1].start()
    for copy in written:
        copy.wait()


def inside(early, codes, raw):
    count, depth = raw.shape[0], raw.shape[1] // 4 * 3
    anywhere = pl.BlockSpec(memory_space=pl.ANY)
    return pl.pallas_call(
        functools.partial(inside_kernel, early),
        out_shape=spec(count, depth),
        in_specs=[anywhere] * 2,
        out_specs=anywhere,
        scratch_shapes=[
            pltpu.VMEM(codes.shape, bf16),
            pltpu.VMEM(raw.shape, bf16),
            pltpu.VMEM((count, depth), bf16),
            pltpu.SemaphoreType.DMA((2,)),
            pltpu.SemaphoreType.DMA((2,)),
        ],
        compiler_params=pltpu.CompilerParams(vmem_limit_bytes=VMEM_ALL),
        cost_estimate=LIGHT,
        name="inside",
    )(codes, raw)


def attend_kernel(early, rows, *refs):
    inputs, out, rest = refs[:7], refs[7], refs[8:]
    held, (state0, state1, sems, out_sems) = rest[:7], rest[7:]
    pairs = list(zip(inputs[:5], held[:5]))
    count = held[6].shape[0]
    for low in range(0, count, BLK):
        part = slice(low, low + BLK)
        pairs += [(source.at[part], target.at[part]) for source, target in zip(inputs[5:], held[5:])]
    copies = fetch(pairs, sems)
    for copy in copies[:5]:
        copy.wait()
    codes, raw, made = held[0], held[5], held[6]
    width = made.shape[1] // 3
    enter_states(float(early), rows, *held[:5], state0, state1)
    written = []
    for i, low in enumerate(range(0, count, BLK)):
        high = low + BLK
        begins, ends, state = (0, early, state0) if high <= early else (early, count, state1)
        for copy in copies[5 + 2 * i : 7 + 2 * i]:
            copy.wait()
        where = lax.broadcasted_iota(jnp.int32, (BLK, HDIM), 0).astype(f32) + (low - begins)
        for head in range(width // HDIM):
            rate = jnp.exp2(-0.5 * codes[head : head + 1, :].astype(f32))
            lead, lag = jnp.exp(-rate * (where + 1.0)), jnp.exp(-rate * (ends - begins - where))
            k, v, g = (raw[low:high, part * width + head * HDIM : part * width + (head + 1) * HDIM] for part in (1, 2, 3))
            kv = state[head * HDIM : (head + 1) * HDIM, :]
            qg = state[width + head * HDIM : width + (head + 1) * HDIM, :]
            for part, value in enumerate((lead * nt(g, kv), lag * nt(v, qg), lag * nn(k, qg))):
                here = pl.ds(part * width + head * HDIM, HDIM)
                made[low:high, here] = (made[low:high, here].astype(f32) + value).astype(bf16)
        written.append(pltpu.make_async_copy(made.at[low:high], out.at[low:high], out_sems.at[i]))
        written[-1].start()
    for copy in written:
        copy.wait()


def attend(early, rows, codes, mine, theirs, other, local, raw, made):
    operands = (codes, mine, theirs, other, local, raw, made)
    state = pltpu.VMEM((2 * other.shape[1] * HDIM + codes.shape[0], HDIM), bf16)
    anywhere = pl.BlockSpec(memory_space=pl.ANY)
    return pl.pallas_call(
        functools.partial(attend_kernel, early, rows),
        out_shape=spec(*made.shape),
        in_specs=[anywhere] * 7,
        out_specs=anywhere,
        scratch_shapes=[pltpu.VMEM(a.shape, a.dtype) for a in operands]
        + [state, state, pltpu.SemaphoreType.DMA((5 + 2 * (made.shape[0] // BLK),)), pltpu.SemaphoreType.DMA((made.shape[0] // BLK,))],
        compiler_params=pltpu.CompilerParams(vmem_limit_bytes=VMEM_ALL),
        cost_estimate=LIGHT,
        name="attend",
    )(*operands)


OWN_STEPS = 4


def own_kernel(done, wq, wk, wv, out, w, sems):
    y = lax.axis_index("head")
    cols, width = w.shape[1:]
    part = cols // OWN_STEPS
    pairs = []
    for step in range(OWN_STEPS):
        begins = pl.multiple_of(y * cols + step * part, part)
        pairs += [(ref.at[pl.ds(begins, part)], w.at[i, pl.ds(step * part, part)]) for i, ref in enumerate((wq, wk, wv))]
    copies = fetch(pairs, sems)
    for step in range(OWN_STEPS):
        for copy in copies[3 * step : 3 * step + 3]:
            copy.wait()
        here = slice(step * part, (step + 1) * part)
        total = None
        for i in range(3):
            term = nt(done[:, i * width : (i + 1) * width], w[i, here])
            total = term if total is None else total + term
        out[:, here] = total.astype(bf16)


def project_own(done, weights):
    rows = done.shape[0]
    cols, width = weights[0].shape[0] // 4, weights[0].shape[1]
    return pl.pallas_call(
        own_kernel,
        out_shape=spec(rows, cols),
        in_specs=whole(1) + [pl.BlockSpec(memory_space=pl.ANY)] * 3,
        out_specs=pl.BlockSpec(memory_space=pltpu.VMEM),
        scratch_shapes=[pltpu.VMEM((3, cols, width), bf16), pltpu.SemaphoreType.DMA((3 * OWN_STEPS,))],
        compiler_params=params(),
        cost_estimate=LIGHT,
        name="project_own",
    )(done, *weights)


def arrange_kernel(*refs):
    *blocks, out = refs
    z, x, c = spot()
    outer = jnp.where(c == 0, z, x)
    share = blocks[0].shape[1]
    for far, block in enumerate(blocks):
        at = pl.multiple_of(lax.rem(outer + 4 - far, 4) * share, share)
        for src in range(3):
            out[src, pl.ds(at, share)] = block[src]


def arrange(blocks):
    srcs, share, depth = blocks[0].shape
    return pl.pallas_call(
        arrange_kernel,
        out_shape=spec(srcs, 4 * share, depth),
        in_specs=whole(4),
        out_specs=pl.BlockSpec(memory_space=pltpu.VMEM),
        compiler_params=params(),
        cost_estimate=LIGHT,
        name="arrange",
    )(*blocks)


def column_tiles(tables, cores):
    z, x, c = spot()
    for table, mirrored in zip(tables, cores):
        core = 1 - c if mirrored else c
        half = table.shape[1]
        for start in range(0, half, BLK):
            yield table, slice(start, start + BLK), pl.ds(pl.multiple_of(core * half + start, BLK), BLK)


def others_kernel(spans, cores, *refs):
    z, x, c = spot()
    parts, refs = refs[: len(spans)], refs[len(spans) :]
    tables, (partial, out) = refs[: len(cores)], refs[len(cores) :]
    for table, inside, at in column_tiles(tables, cores):
        total = partial[:, at].astype(f32)
        for (src, _), part in zip(spans, parts):
            total = total + nt(part[...], table[jnp.where(c == 1, src - 1, 2 - src), inside])
        out[:, at] = total.astype(bf16)


def project_others(parts, tables, mirrored, partial):
    spans = tuple(part[:2] for part in parts)
    operands = [*[part[2] for part in parts], *tables, partial]
    return pl.pallas_call(
        functools.partial(others_kernel, spans, mirrored),
        out_shape=spec(*partial.shape),
        in_specs=whole(len(operands)),
        out_specs=pl.BlockSpec(memory_space=pltpu.VMEM),
        input_output_aliases={len(operands) - 1: 0},
        compiler_params=params(),
        cost_estimate=LIGHT,
        name="project_others",
    )(*operands)


def last_kernel(spans, cores, *refs):
    parts, refs = refs[: len(spans)], refs[len(spans) :]
    tables, refs = refs[: len(cores)], refs[len(cores) :]
    partial, refs = refs[0], refs[1:]
    out, tiles, sems = refs[-3:]
    made = []
    src, rows = spans[0][0], parts[0].shape[0]
    together = jnp.concatenate([part[...] for part in parts], axis=0)
    for table, inside, at in column_tiles(tables, cores):
        product = nt(together, table[src - 1, inside])
        for i, (_, start) in enumerate(spans):
            total = partial[start : start + rows, at].astype(f32) + product[i * rows : (i + 1) * rows]
            slot = len(made)
            tiles[slot] = total.astype(bf16)
            made.append(pltpu.make_async_copy(tiles.at[slot], out.at[pl.ds(start, rows), at], sems.at[slot]))
            made[-1].start()
    for copy in made:
        copy.wait()


def project_last(parts, tables, mirrored, partial, held=None):
    rows = parts[0][2].shape[0]
    count = len(parts) * len(tables) * tables[0].shape[1] // BLK
    spans = tuple(part[:2] for part in parts)
    operands = [*[part[2] for part in parts], *tables, partial] + ([] if held is None else [held])
    anywhere = pl.BlockSpec(memory_space=pl.ANY)
    return pl.pallas_call(
        functools.partial(last_kernel, spans, mirrored),
        out_shape=spec(*partial.shape),
        in_specs=whole(len(parts) + len(tables) + 1) + ([] if held is None else [anywhere]),
        out_specs=anywhere,
        scratch_shapes=[pltpu.VMEM((count, rows, BLK), bf16), pltpu.SemaphoreType.DMA((count,))],
        input_output_aliases={} if held is None else {len(operands) - 1: 0},
        compiler_params=params(),
        cost_estimate=LIGHT,
        name="project_last",
    )(*operands)


def turn(a, by):
    return lax.ppermute(a, "head", [(i, (i + by) % 4) for i in range(4)])


def swing(a, by):
    pairs = []
    for seq in range(32):
        for y in range(4):
            to = (y + (by if seq % 2 == 1 else -by)) % 4
            pairs.append((seq * 4 + y, seq * 4 + to))
    return lax.ppermute(a, ("seq", "head"), pairs)


def move(a, where):
    pairs = [(place(z, x, c), place(*where(z, x, c))) for z in range(4) for x in range(4) for c in range(2)]
    return lax.ppermute(a, "seq", pairs)


def across(a):
    return move(a, lambda z, x, c: (z, x, 1 - c))


CHIPS = [[place(z, x, c) for z in range(4) for x in range(4)] for c in range(2)]
def major(a, by):
    return move(a, lambda z, x, c: (z + by, x, c) if c == 0 else (z, x + by, c))


def tie(*groups):
    return lax.optimization_barrier(groups)


def shards(queries, key_rows, value_rows, grad_out, accepted, decay_code, w_query, w_key, w_value):
    heads = decay_code.shape[0]
    count = queries.shape[0]
    rows = float(count)
    weights = (w_query, w_key, w_value)
    raw, codes, local, message, *sent = begin(
        queries, key_rows, value_rows, grad_out, accepted, decay_code, weights, EARLY
    )
    other = across(message)
    leaving = join(rows, codes, message, other)
    share = [turn(sent[0], 1), turn(sent[1], -1), turn(sent[2], 2)]
    arrived = lax.all_to_all(leaving, "seq", 0, 0, axis_index_groups=CHIPS)
    held, leaving = tie((codes, raw), leaving)
    arrived, made = tie(arrived, inside(EARLY, *held))
    chip_state = gather(rows, decay_code, arrived)
    theirs = across(chip_state)
    done = attend(EARLY, rows, codes, chip_state, theirs, other, local, raw, made)
    done, *share = tie(done, *share)
    former, latter = swing(done, 1), swing(done, -1)
    total = project_own(done, weights)
    former, latter, total = tie(former, latter, total)
    share = jnp.stack(share)
    half = [share] + [major(share, by) for by in (1, 2, 3)]
    half, _, _ = tie(half, former, latter)
    half = arrange(half)
    other_half = across(half)
    far = []
    for start in range(0, count // 2, CHUNK):
        far.append((3, start, swing(former[start : start + CHUNK], 1)))
        start += count // 2
        far.append((3, start, swing(latter[start : start + CHUNK], -1)))
    sides = (1, 0, former), (2, 0, latter)
    total = project_others(sides, (half,), (False,), total)
    total = project_others(sides, (other_half,), (True,), total)
    out = None
    for i in range(0, len(far), 2):
        out = project_last(far[i : i + 2], (half, other_half), (False, True), total, out)
    return out


def solution(mesh):
    in_specs = (P("seq", "head"),) * 4 + (P("seq"), P("head")) + (P(None, "head"),) * 3
    return jax.shard_map(shards, mesh=mesh, in_specs=in_specs, out_specs=P("seq", "head"), check_vma=False)
```
